32 devices in a mesh: ctx: 8 (over z, x), seq: 4 (over y, core).
Axes of the slice: x: 2, y: 2, z: 4, core: 2. Of those that a mesh axis runs over, the one named last changes fastest.
Arguments:
- queries: bfloat16 [4096, 8192], P('ctx', 'seq'), may hold values from -0.5 to 0.5
- keys: bfloat16 [4096, 8192], P('ctx', 'seq'), may hold values from -0.5 to 0.5
- values: bfloat16 [4096, 8192], P('ctx', 'seq'), may hold values from -6 to 6
- out_grad: bfloat16 [4096, 8192], P('ctx', 'seq'), may hold values from -0.5 to 0.5
Outputs:
- attended: bfloat16 [4096, 8192], P('ctx', 'seq')
- query_grad: bfloat16 [4096, 8192], P('ctx', 'seq')
- key_grad: bfloat16 [4096, 8192], P('ctx', 'seq')
- value_grad: bfloat16 [4096, 8192], P('ctx', 'seq')
The draws below stay inside these ranges and needn't reach their ends.
All inputs are finite; a program needn't handle non-finite values.
Results may differ from the reference program's by a relative error of at most 0.0049.
Values sent between devices are 32-bit elements; how exact they have to be, the bound alone decides.
No kernel may reach another device: no remote copies, remote signals or barrier semaphores. Data moves between devices by JAX's collectives and lax.ppermute only.
A program may use at most 128 MiB of HBM per device.

```python
import jax
import jax.numpy as jnp
from jax import lax

H = 64
DH = 128
BLOCK = 128
TOKENS = 4096


def level_of(stream_key, extent, shards, low, high):
    def one(dim, blocks):
        heights = jax.random.uniform(jax.random.fold_in(jax.random.fold_in(stream_key, 6), dim), (blocks,), jnp.float32, low / len(shards), high / len(shards))
        return jnp.repeat(jnp.exp(heights), extent[dim] // blocks).reshape((-1,) + (1,) * (len(extent) - dim - 1))

    loudness = one(*shards[0])
    for cut in shards[1:]:
        loudness = loudness * one(*cut)
    return loudness


def gaussian(own_key, extent, scale, limit, pieces=(), dtype=jnp.bfloat16):
    entries = scale * jax.random.normal(own_key, extent, jnp.float32)
    if pieces:
        entries = entries * level_of(own_key, extent, pieces, -0.22, 0.18)
    return jnp.clip(entries, -limit, limit).astype(dtype)


def setup_inputs(seed: int = 0) -> dict:
    key_of = jax.random.split(jax.random.key(seed), 5)
    queries = gaussian(key_of[0], (TOKENS, H * DH), (1.0 / (TOKENS * DH) ** 0.25), 0.5, ((0, 8), (1, 4)))
    keys = gaussian(key_of[1], (TOKENS, H * DH), (1.0 / (TOKENS * DH) ** 0.25), 0.5, ((0, 8), (1, 4)))
    values = gaussian(key_of[2], (TOKENS, H * DH), 1.0, 6.0, ((0, 8), (1, 4)))
    out_grad = gaussian(key_of[3], (TOKENS, H * DH), (1.0 / (TOKENS * DH) ** 0.25), 0.5, ((0, 8), (1, 4)))
    return dict(queries=queries, keys=keys, values=values, out_grad=out_grad)


def block_terms(qb, kb, vb, gb):
    qf = qb.astype(jnp.float32)
    kf = kb.astype(jnp.float32)
    vf = vb.astype(jnp.float32)
    gf = gb.astype(jnp.float32)
    count = qb.shape[0]
    rows = lax.broadcasted_iota(jnp.int32, (count, count), 0)
    cols = lax.broadcasted_iota(jnp.int32, (count, count), 1)
    causal = (cols <= rows)[None]
    attn = jnp.where(causal, jnp.einsum("thi,shi->hts", qf, kf), 0.0).astype(jnp.bfloat16).astype(jnp.float32)
    grads = jnp.where(causal, jnp.einsum("thj,shj->hts", gf, vf), 0.0).astype(jnp.bfloat16).astype(jnp.float32)
    return qf, kf, vf, gf, attn, grads


def reference(queries, keys, values, out_grad):
    blocks = TOKENS // BLOCK
    shape = (blocks, BLOCK, H, DH)
    qs = queries.reshape(shape)
    ks = keys.reshape(shape)
    vs = values.reshape(shape)
    gs = out_grad.reshape(shape)

    def forward(carry, items):
        qb, kb, vb, gb = items
        qf, kf, vf, gf, attn, grads = block_terms(qb, kb, vb, gb)
        prefix_low = carry.astype(jnp.bfloat16).astype(jnp.float32)
        attended = jnp.einsum("hts,shj->thj", attn, vf) + jnp.einsum("thi,hij->thj", qf, prefix_low)
        query_grad = jnp.einsum("hts,shi->thi", grads, kf) + jnp.einsum("thj,hij->thi", gf, prefix_low)
        kv_block = jnp.einsum("thi,thj->hij", kf, vf)
        return carry + kv_block, (attended.astype(jnp.bfloat16), query_grad.astype(jnp.bfloat16))

    def backward(carry, items):
        qb, kb, vb, gb = items
        qf, kf, vf, gf, attn, grads = block_terms(qb, kb, vb, gb)
        suffix_low = carry.astype(jnp.bfloat16).astype(jnp.float32)
        key_grad = jnp.einsum("hts,thi->shi", grads, qf) + jnp.einsum("shj,hij->shi", vf, suffix_low)
        value_grad = jnp.einsum("hts,thj->shj", attn, gf) + jnp.einsum("shi,hij->shj", kf, suffix_low)
        qg_block = jnp.einsum("thi,thj->hij", qf, gf)
        return carry + qg_block, (key_grad.astype(jnp.bfloat16), value_grad.astype(jnp.bfloat16))

    start = jnp.zeros((H, DH, DH), jnp.float32)
    _, (attended, query_grad) = lax.scan(forward, start, (qs, ks, vs, gs))
    _, (key_grad, value_grad) = lax.scan(backward, start, (qs, ks, vs, gs), reverse=True)
    flat = (TOKENS, H * DH)
    return (attended.reshape(flat), query_grad.reshape(flat), key_grad.reshape(flat), value_grad.reshape(flat))
```

```python
import functools

import jax
import jax.numpy as jnp
from jax import lax
from jax.experimental import pallas as pl
from jax.experimental.pallas import tpu as pltpu
from jax.sharding import PartitionSpec as P

DH = 128
BLOCK = 128
F32 = jnp.float32
BF16 = jnp.bfloat16
ROWS = ((0,), (0,))
LANES = ((1,), (1,))
PLAIN = ((1,), (0,))


def dot(a, b, dims):
    return lax.dot_general(a, b, (dims, ((), ())), preferred_element_type=F32)


def states_kernel(q_ref, k_ref, v_ref, g_ref, out_ref):
    for h in range(out_ref.shape[1]):
        cols = slice(h * DH, (h + 1) * DH)
        out_ref[0, h] = dot(k_ref[:, cols], v_ref[:, cols], ROWS)
        out_ref[1, h] = dot(q_ref[:, cols], g_ref[:, cols], ROWS)


def states_of(arrays, first, size, step):
    rows = arrays[0].shape[0]
    spec = pl.BlockSpec((rows, step * DH), lambda i: (0, first // step + i))
    return pl.pallas_call(
        states_kernel,
        grid=(size // step,),
        in_specs=[spec] * 4,
        out_specs=pl.BlockSpec((2, step, DH, DH), lambda i: (0, i, 0, 0)),
        out_shape=jax.ShapeDtypeStruct((2, size, DH, DH), F32),
        name="states",
    )(*arrays)


def outputs_kernel(step, *refs):
    q_ref, k_ref, v_ref, g_ref, before_ref, after_ref = refs[:6]
    attended_ref, query_ref, key_ref, value_ref = refs[-4:]
    nblocks = q_ref.shape[0] // BLOCK
    rows = lax.broadcasted_iota(jnp.int32, (BLOCK, BLOCK), 0)
    cols = lax.broadcasted_iota(jnp.int32, (BLOCK, BLOCK), 1)
    causal = cols <= rows

    def scores(a, b):
        return jnp.where(causal, dot(a, b, LANES), 0.0).astype(BF16)

    for h in range(step):
        lanes = slice(h * DH, (h + 1) * DH)
        at = [(slice(b * BLOCK, (b + 1) * BLOCK), lanes) for b in range(nblocks)]
        lows = []
        state = before_ref[h]
        for b in range(nblocks):
            lows.append(state.astype(BF16))
            if b < nblocks - 1:
                state = state + dot(k_ref[at[b]], v_ref[at[b]], ROWS)
        for b in range(nblocks):
            q, k, v, g = q_ref[at[b]], k_ref[at[b]], v_ref[at[b]], g_ref[at[b]]
            low = lows[b]
            attn, grads = scores(q, k), scores(g, v)
            attended_ref[at[b]] = dot(
                jnp.concatenate([attn, q], 1), jnp.concatenate([v, low], 0), PLAIN
            ).astype(BF16)
            query_ref[at[b]] = dot(
                jnp.concatenate([grads, g], 1), jnp.concatenate([k, low.T], 0), PLAIN
            ).astype(BF16)
        state = after_ref[h]
        for b in reversed(range(nblocks)):
            q, k, v, g = q_ref[at[b]], k_ref[at[b]], v_ref[at[b]], g_ref[at[b]]
            low = state.astype(BF16)
            if b > 0:
                state = state + dot(q, g, ROWS)
            attn, grads = scores(q, k), scores(g, v)
            key_ref[at[b]] = dot(
                jnp.concatenate([grads.T, v], 1), jnp.concatenate([q, low.T], 0), PLAIN
            ).astype(BF16)
            value_ref[at[b]] = dot(
                jnp.concatenate([attn.T, k], 1), jnp.concatenate([g, low], 0), PLAIN
            ).astype(BF16)


def outputs_of(arrays, before, after, outs, first, size, step):
    rows = arrays[0].shape[0]
    spec = pl.BlockSpec((rows, step * DH), lambda i: (0, first // step + i))
    state = pl.BlockSpec((step, DH, DH), lambda i: (i, 0, 0))
    held = () if outs is None else tuple(outs)
    return pl.pallas_call(
        functools.partial(outputs_kernel, step),
        grid=(size // step,),
        in_specs=[spec] * 4 + [state] * 2 + [pl.BlockSpec(memory_space=pl.ANY)] * len(held),
        out_specs=[spec] * 4,
        out_shape=[jax.ShapeDtypeStruct(a.shape, BF16) for a in arrays],
        input_output_aliases={6 + i: i for i in range(len(held))},
        name="outputs",
    )(*arrays, before, after, *held)


def any_of(place, places):
    return functools.reduce(jnp.logical_or, [place == p for p in places])


def body(*arrays):
    heads = arrays[0].shape[1] // DH
    runs = lax.axis_size("ctx")
    chain = runs // 2
    place = lax.axis_index("ctx")
    row, column = place // 2, place % 2
    parts = 4
    size = heads // parts
    own = [None] * parts
    for p in (2, 0, 1, 3):
        own[p] = states_of(arrays, p * size, size, min(size, 2))
    pair = [(r, r ^ 1) for r in range(runs)]
    swapped = [None] * parts
    swapped[2] = lax.ppermute(own[2], "ctx", pair)
    swapped[3] = lax.ppermute(own[3], "ctx", pair)

    def along(p):
        return own[p] if p < 2 else own[p] + swapped[p]

    carried = [along(p) for p in range(parts)]
    got = {}

    def arrival(p, z, way):
        if way == 0:
            return None if z == 0 else ((z - 1) % 2, p + z - 1)
        return None if z == chain - 1 else (z % 2, p + chain - 2 - z)

    def chained(p, way):
        total = jnp.zeros_like(own[p][0])
        by_key = {}
        for z in range(chain):
            key = arrival(p, z, way)
            if key is not None:
                by_key.setdefault(key, []).append(z)
        for key, places in by_key.items():
            total = jnp.where(any_of(row, places), got[key], total)
        return total

    for slot in range(parts + chain - 2):
        for parity in range(2):
            groups, perm = {}, []
            for link in range(parity, chain - 1, 2):
                for way, p, z, to in ((0, slot - link, link, link + 1), (1, slot - (chain - 2 - link), link + 1, link)):
                    if 0 <= p < parts:
                        groups.setdefault((p, arrival(p, z, way)), {}).setdefault(way, []).append(z)
                        perm += [(2 * z + c, 2 * to + c) for c in range(2)]
            if not perm:
                continue
            payload = None
            for (p, key), ways in groups.items():
                if len(ways) == 2:
                    value = jnp.where(any_of(row, ways[0]), carried[p][0], carried[p][1])
                else:
                    value = carried[p][next(iter(ways))]
                if key is not None:
                    value = value + got[key]
                places = [z for zs in ways.values() for z in zs]
                payload = value if payload is None else jnp.where(any_of(row, places), value, payload)
            got[parity, slot] = lax.ppermute(payload, "ctx", perm)

    outs = None
    for p in (0, 2, 1, 3):
        before, after = chained(p, 0), chained(p, 1)
        if p < 2:
            first = jnp.where(column == 0, own[p][0], 0.0)
            second = jnp.where(column == 1, own[p][1], 0.0)
            swapped[p] = lax.ppermute(jnp.stack([before + first, after + second]), "ctx", pair)
            before, after = before + swapped[p][0], after + swapped[p][1]
        else:
            before = before + jnp.where(column == 1, swapped[p][0], 0.0)
            after = after + jnp.where(column == 0, swapped[p][1], 0.0)
        outs = outputs_of(arrays, before, after, outs, p * size, size, 1)
    return tuple(outs)


def solution(mesh):
    spec = P("ctx", "seq")
    return jax.shard_map(body, mesh=mesh, in_specs=(spec,) * 4, out_specs=(spec,) * 4, check_vma=False)
```

```python
import functools

import jax
import jax.numpy as jnp
from jax import lax
from jax.experimental import pallas as pl
from jax.experimental.pallas import tpu as pltpu
from jax.sharding import PartitionSpec as P

DH = 128
F32 = jnp.float32
BF16 = jnp.bfloat16
ROWS = ((0,), (0,))
LANES = ((1,), (1,))
PLAIN = ((1,), (0,))
VMEM = pl.BlockSpec(memory_space=pltpu.VMEM)
HBM = pl.BlockSpec(memory_space=pltpu.HBM)
PARAMS = pltpu.CompilerParams(vmem_limit_bytes=8 << 20)


def dot(a, b, dims):
    return lax.dot_general(a, b, (dims, ((), ())), preferred_element_type=F32)


def kept(arrays):
    return [pltpu.with_memory_space_constraint(a, pltpu.VMEM) for a in arrays]


def any_of(place, places):
    return functools.reduce(jnp.logical_or, [place == p for p in places])


def spot():
    place = lax.axis_index("ctx")
    return place // 2, place % 2


def load_kernel(first, chain, q_hbm, k_hbm, v_hbm, g_hbm, *refs):
    q_ref, k_ref, v_ref, g_ref, state_ref, opening_ref, sems = refs[-7:]
    size = state_ref.shape[1]
    moves = []
    for h in range(size):
        here, there = pl.ds(h * DH, DH), pl.ds((first + h) * DH, DH)
        pairs = ((k_hbm, k_ref), (v_hbm, v_ref), (q_hbm, q_ref), (g_hbm, g_ref))
        for i, (src, dst) in enumerate(pairs):
            moves.append(pltpu.make_async_copy(src.at[:, there], dst.at[:, here], sems.at[h, i]))
    for move in moves:
        move.start()
    row, _ = spot()
    for h in range(size):
        for move in moves[4 * h : 4 * h + 4]:
            move.wait()
        cols = slice(h * DH, (h + 1) * DH)
        kv, qg = dot(k_ref[:, cols], v_ref[:, cols], ROWS), dot(q_ref[:, cols], g_ref[:, cols], ROWS)
        state_ref[0, h], state_ref[1, h] = kv, qg
        opening_ref[h] = jnp.where(row < chain // 2, kv, qg)


def load(arrays, first, size, chain, after):
    rows = arrays[0].shape[0]
    *run, state, opening = pl.pallas_call(
        functools.partial(load_kernel, first, chain),
        in_specs=[HBM] * 4 + [VMEM] * len(after),
        out_specs=[VMEM] * 6,
        out_shape=[pltpu.VMEM((rows, size * DH), BF16)] * 4
        + [pltpu.VMEM((2, size, DH, DH), F32), pltpu.VMEM((size, DH, DH), F32)],
        scratch_shapes=[pltpu.SemaphoreType.DMA((size, 4))],
        compiler_params=PARAMS,
        name="load",
    )(*[pltpu.with_memory_space_constraint(a, pltpu.HBM) for a in arrays], *kept(after))
    return run, state, opening


def within_kernel(tile, *refs):
    q_ref, k_ref, v_ref, g_ref = refs[:4]
    attended_ref, query_ref, key_ref, value_ref = refs[-4:]
    rows, width = q_ref.shape
    count = rows // tile
    causal = lax.broadcasted_iota(jnp.int32, (tile, tile), 1) <= lax.broadcasted_iota(jnp.int32, (tile, tile), 0)

    def head(h, _):
        lanes = pl.ds(pl.multiple_of(h * DH, DH), DH)
        at = [pl.ds(i * tile, tile) for i in range(count)]
        q, k, v, g = ([ref[a, lanes] for a in at] for ref in (q_ref, k_ref, v_ref, g_ref))
        attn, grads = {}, {}
        for i in range(count):
            for j in range(i + 1):
                a, b = dot(q[i], k[j], LANES), dot(g[i], v[j], LANES)
                if i == j:
                    a, b = jnp.where(causal, a, 0.0), jnp.where(causal, b, 0.0)
                attn[i, j], grads[i, j] = a.astype(BF16), b.astype(BF16)
        for i in range(count):
            attended_ref[at[i], lanes] = sum(dot(attn[i, j], v[j], PLAIN) for j in range(i + 1))
            query_ref[at[i], lanes] = sum(dot(grads[i, j], k[j], PLAIN) for j in range(i + 1))
        for j in range(count):
            key_ref[at[j], lanes] = sum(dot(grads[i, j], q[i], ROWS) for i in range(j, count))
            value_ref[at[j], lanes] = sum(dot(attn[i, j], g[i], ROWS) for i in range(j, count))
        return 0

    lax.fori_loop(0, width // DH, head, 0, unroll=2 if width > DH else 1)


def within(run, after):
    rows, width = run[0].shape
    return pl.pallas_call(
        functools.partial(within_kernel, min(rows, 256)),
        in_specs=[VMEM] * (4 + len(after)),
        out_specs=[VMEM] * 4,
        out_shape=[pltpu.VMEM((rows, width), F32)] * 4,
        compiler_params=PARAMS,
        name="within",
    )(*kept(run), *kept(after))


def mix(function, shape, arrays, after, name):
    def kernel(*refs):
        row, column = spot()
        function(row, column, refs[: len(arrays)], refs[-1])

    return pl.pallas_call(
        kernel,
        in_specs=[VMEM] * (len(arrays) + len(after)),
        out_specs=VMEM,
        out_shape=pltpu.VMEM(shape, F32),
        compiler_params=PARAMS,
        name=name,
    )(*kept(arrays), *kept(after))


def across_kernel(total, count, *refs):
    q_ref, k_ref, v_ref, g_ref = refs[:4]
    parts = refs[4:8]
    sources = refs[8 : 8 + count]
    *outs, token_ref = refs[-5:]
    row, column = spot()
    head = pl.program_id(0)
    there = pl.ds(pl.multiple_of(head * DH, DH), DH)
    before, after = (x.astype(BF16) for x in total(row, column, sources, head))
    terms = (
        dot(q_ref[:, there], before, PLAIN),
        dot(g_ref[:, there], before, LANES),
        dot(v_ref[:, there], after, LANES),
        dot(k_ref[:, there], after, PLAIN),
    )
    for out, part, term in zip(outs, parts, terms, strict=True):
        out[...] = (part[:, there] + term).astype(BF16)
    token_ref[...] = jnp.zeros_like(token_ref)


def across(total, run, parts, sources, outs, shape, first, size, after):
    held = () if outs is None else tuple(outs)
    spec = pl.BlockSpec((shape[0], DH), lambda i: (0, first + i))
    fixed = 8 + len(sources)
    *outs, token = pl.pallas_call(
        functools.partial(across_kernel, total, len(sources)),
        grid=(size,),
        in_specs=[VMEM] * fixed + [HBM] * len(held) + [VMEM] * len(after),
        out_specs=[spec] * 4 + [VMEM],
        out_shape=[jax.ShapeDtypeStruct(shape, BF16)] * 4 + [pltpu.VMEM((8, DH), F32)],
        input_output_aliases={fixed + i: i for i in range(len(held))},
        compiler_params=PARAMS,
        name="across",
    )(*kept(run), *kept(parts), *kept(sources), *held, *kept(after))
    return outs, token


def body(*arrays):
    heads = arrays[0].shape[1] // DH
    runs, groups_of_heads = lax.axis_size("ctx"), lax.axis_size("seq")
    chain = runs // 2
    parts = 4
    size = heads // parts
    shape = (size, DH, DH)
    run, own, opening, local = ([None] * parts for _ in range(4))
    swapped = {}
    got = {}
    last = []
    pair = [(r, r ^ 1) for r in range(runs)]

    def swap(parity):
        perm = []
        for r in range(runs):
            z, c = r // 2, r % 2
            mate = z + 1 if z % 2 == parity else z - 1
            for s in range(groups_of_heads):
                if 0 <= mate < chain:
                    to = (2 * mate + c) * groups_of_heads + s
                else:
                    to = r * groups_of_heads + (s ^ 1)
                perm.append((r * groups_of_heads + s, to))
        return perm

    def arrival(p, z, way):
        if way == 0:
            return None if z == 0 else ((z - 1) % 2, p + z - 1)
        return None if z == chain - 1 else (z % 2, p + chain - 2 - z)

    def bring(p):
        run[p], own[p], opening[p] = load(arrays, p * size, size, chain, last)
        last[:] = [own[p]]

    def inside(p):
        local[p] = within(run[p], last)
        last[:] = [local[p][0]]

    def trade(p):
        if p >= 2:
            swapped[p] = lax.ppermute(own[p], "ctx", pair)
            return
        keys = sorted({arrival(p, z, way) for z in range(chain) for way in range(2)} - {None})

        def function(row, column, refs, out):
            for way, near in ((0, 0), (1, 1)):
                value = jnp.where(column == near, refs[0][way], 0.0)
                out[way] = value + chained(p, way, row, refs[1:], keys, slice(None))

        payload = mix(function, (2,) + shape, [own[p]] + [got[k] for k in keys], last, "trade")
        last[:] = [payload]
        swapped[p] = lax.ppermute(payload, "ctx", pair)

    def chained(p, way, row, refs, keys, at):
        total = jnp.zeros(refs[0][at].shape, F32)
        for key, ref in zip(keys, refs, strict=True):
            places = [z for z in range(chain) if arrival(p, z, way) == key]
            if places:
                total = jnp.where(any_of(row, places), ref[at], total)
        return total

    def hop(parity, slot):
        groups = {}
        for link in range(parity, chain - 1, 2):
            for way, p, z in ((0, slot - link, link), (1, slot - (chain - 2 - link), link + 1)):
                if 0 <= p < parts:
                    groups.setdefault((p, arrival(p, z, way)), ([], []))[way].append(z)
        if not groups:
            return
        names = []

        def use(name):
            if name not in names:
                names.append(name)

        for p, key in groups:
            use(("own", p))
            if p >= 2:
                use(("swapped", p))
            if key is not None:
                use(("got", key))
        tables = {"own": own, "swapped": swapped, "got": got}
        values = [tables[kind][key] for kind, key in names]

        def function(row, column, refs, out):
            refs = dict(zip(names, refs, strict=True))
            payload = None
            for (p, key), (up, down) in groups.items():
                def state(way):
                    value = refs["own", p][way]
                    return value + refs["swapped", p][way] if p >= 2 else value

                if up and down:
                    value = jnp.where(any_of(row, up), state(0), state(1))
                else:
                    value = state(0 if up else 1)
                if key is not None:
                    value = value + refs["got", key][...]
                payload = value if payload is None else jnp.where(any_of(row, up + down), value, payload)
            out[...] = payload

        plain = len(groups) == 1 and next(iter(groups)) in ((0, None), (1, None))
        if plain and chain > 2:
            payload = opening[next(iter(groups))[0]]
        else:
            payload = mix(function, shape, values, last, "hop")
            last[:] = [payload]
        got[parity, slot] = lax.ppermute(payload, ("ctx", "seq"), swap(parity))

    outs = [None]

    def finish(p):
        keys = sorted({arrival(p, z, way) for z in range(chain) for way in range(2)} - {None})

        def total(row, column, refs, head):
            for way, far in ((0, 1), (1, 0)):
                value = refs[0][way, head]
                if p >= 2:
                    value = jnp.where(column == far, value, 0.0)
                yield value + chained(p, way, row, refs[1:], keys, head)

        outs[0], token = across(
            total, run[p], local[p], [swapped[p]] + [got[k] for k in keys], outs[0], arrays[0].shape, p * size, size, last
        )
        last[:] = [token]

    bring(2)
    trade(2)
    bring(0)
    hop(0, 0)
    bring(3)
    trade(3)
    bring(1)
    hop(0, 1)
    if chain == 4:
        inside(2)
        hop(1, 1)
        inside(0)
        inside(1)
        hop(0, 2)
        hop(1, 2)
        inside(3)
        trade(0)
        hop(1, 3)
        hop(0, 3)
        hop(0, 4)
        hop(1, 4)
        trade(1)
        finish(0)
        hop(0, 5)
        finish(2)
        finish(3)
        finish(1)
    else:
        for p in range(parts):
            inside(p)
        for slot in range(parts + chain - 2):
            for parity in range(2):
                if (parity, slot) not in got:
                    hop(parity, slot)
        trade(0)
        trade(1)
        for p in (2, 3, 0, 1):
            finish(p)
    return tuple(outs[0])


def solution(mesh):
    spec = P("ctx", "seq")
    return jax.shard_map(body, mesh=mesh, in_specs=(spec,) * 4, out_specs=(spec,) * 4, check_vma=False)
```

```python
import functools

import jax
import jax.numpy as jnp
from jax import lax
from jax.experimental import pallas as pl
from jax.experimental.pallas import tpu as pltpu
from jax.sharding import PartitionSpec as P

DH = 128
F32 = jnp.float32
BF16 = jnp.bfloat16
ROWS = ((0,), (0,))
LANES = ((1,), (1,))
PLAIN = ((1,), (0,))
VMEM = pl.BlockSpec(memory_space=pltpu.VMEM)
HBM = pl.BlockSpec(memory_space=pltpu.HBM)
ACROSS_ROWS = 256
ORDER = (
    "L20", "X2", "E0", "L13", "X3", "O1", "E1", "W20", "W21", "W00", "E2", "W01", "O2", "W10",
    "W11", "X0", "O3", "E3", "W30", "W31", "E4", "O4", "X1", "A0", "E5", "A2", "A3", "A1",
)
PARAMS = pltpu.CompilerParams(vmem_limit_bytes=8 << 20)


def cost(us):
    return pl.CostEstimate(flops=int(us * 1.15e9), transcendentals=0, bytes_accessed=1)


def dot(a, b, dims):
    return lax.dot_general(a, b, (dims, ((), ())), preferred_element_type=F32)


def kept(arrays):
    return [pltpu.with_memory_space_constraint(a, pltpu.VMEM) for a in arrays]


def any_of(place, places):
    return functools.reduce(jnp.logical_or, [place == p for p in places])


def spot():
    place = lax.axis_index("ctx")
    return place // 2, place % 2


def load_kernel(firsts, q_hbm, k_hbm, v_hbm, g_hbm, *refs):
    *refs, sems = refs
    parts = [refs[len(refs) - 5 * (len(firsts) - n) :][:5] for n in range(len(firsts))]
    moves = []
    for n, (first, part) in enumerate(zip(firsts, parts, strict=True)):
        there = pl.ds(first * DH, part[0].shape[1])
        pairs = ((k_hbm, part[1]), (v_hbm, part[2]), (q_hbm, part[0]), (g_hbm, part[3]))
        moves.append([pltpu.make_async_copy(src.at[:, there], dst, sems.at[n, i]) for i, (src, dst) in enumerate(pairs)])
        for move in moves[-1]:
            move.start()
    for part, own in zip(parts, moves, strict=True):
        q_ref, k_ref, v_ref, g_ref, state_ref = part
        size = state_ref.shape[1]
        cols = [slice(h * DH, (h + 1) * DH) for h in range(size)]
        own[0].wait()
        own[1].wait()
        for h in range(size):
            state_ref[0, h] = dot(k_ref[:, cols[h]], v_ref[:, cols[h]], ROWS)
        own[2].wait()
        own[3].wait()
        for h in range(size):
            state_ref[1, h] = dot(q_ref[:, cols[h]], g_ref[:, cols[h]], ROWS)


def load(arrays, firsts, size, after):
    rows = arrays[0].shape[0]
    part = [pltpu.VMEM((rows, size * DH), BF16)] * 4 + [pltpu.VMEM((2, size, DH, DH), F32)]
    return pl.pallas_call(
        functools.partial(load_kernel, firsts),
        in_specs=[HBM] * 4 + [VMEM] * len(after),
        out_specs=[VMEM] * (5 * len(firsts)),
        out_shape=part * len(firsts),
        scratch_shapes=[pltpu.SemaphoreType.DMA((len(firsts), 4))],
        compiler_params=PARAMS,
        cost_estimate=cost(1.5 + 0.5 * len(firsts)),
        name="load",
    )(*[pltpu.with_memory_space_constraint(a, pltpu.HBM) for a in arrays], *kept(after))


def within_kernel(tile, first, *refs):
    q_ref, k_ref, v_ref, g_ref = refs[:4]
    attended_ref, query_ref, key_ref, value_ref = refs[-4:]
    rows, width = attended_ref.shape
    count = rows // tile
    causal = lax.broadcasted_iota(jnp.int32, (tile, tile), 1) <= lax.broadcasted_iota(jnp.int32, (tile, tile), 0)

    @pl.loop(0, width // DH)
    def _(h):
        lanes, source = (pl.ds(pl.multiple_of(n * DH, DH), DH) for n in (h, first + h))
        at = [pl.ds(i * tile, tile) for i in range(count)]
        q, k, v, g = ([ref[a, source] for a in at] for ref in (q_ref, k_ref, v_ref, g_ref))
        attn, grads = {}, {}
        for i in range(count):
            for j in range(i + 1):
                a, b = dot(q[i], k[j], LANES), dot(g[i], v[j], LANES)
                if i == j:
                    a, b = jnp.where(causal, a, 0.0), jnp.where(causal, b, 0.0)
                attn[i, j], grads[i, j] = a.astype(BF16), b.astype(BF16)
        for i in range(count):
            attended_ref[at[i], lanes] = sum(dot(attn[i, j], v[j], PLAIN) for j in range(i + 1))
            query_ref[at[i], lanes] = sum(dot(grads[i, j], k[j], PLAIN) for j in range(i + 1))
        for j in range(count):
            key_ref[at[j], lanes] = sum(dot(grads[i, j], q[i], ROWS) for i in range(j, count))
            value_ref[at[j], lanes] = sum(dot(attn[i, j], g[i], ROWS) for i in range(j, count))


def within(run, first, width, after):
    rows = run[0].shape[0]
    return pl.pallas_call(
        functools.partial(within_kernel, min(rows, 256), first),
        in_specs=[VMEM] * (4 + len(after)),
        out_specs=[VMEM] * 4,
        out_shape=[pltpu.VMEM((rows, width), F32)] * 4,
        compiler_params=PARAMS,
        cost_estimate=cost(1.5),
        name="within",
    )(*kept(run), *kept(after))


def mix(function, shape, arrays, after, name):
    def kernel(*refs):
        row, column = spot()
        function(row, column, refs[: len(arrays)], refs[-1])

    return pl.pallas_call(
        kernel,
        in_specs=[VMEM] * (len(arrays) + len(after)),
        out_specs=VMEM,
        out_shape=pltpu.VMEM(shape, F32),
        compiler_params=PARAMS,
        cost_estimate=cost(3),
        name=name,
    )(*kept(arrays), *kept(after))


def across_kernel(jobs, *refs):
    *outs, token_ref, done_ref, sems = refs[-7:]
    row, column = spot()
    moves, ready = [], []
    for total, first, pieces, count in jobs:
        run, refs = refs[:4], refs[4:]
        parts, refs = [refs[4 * n : 4 * n + 4] for n in range(pieces)], refs[4 * pieces :]
        sources, refs = refs[:count], refs[count:]
        ready.append((run, parts, first, [value.astype(BF16) for value in total(row, column, sources)]))
    for n, (run, parts, first, (before, after)) in enumerate(ready):
        q_ref, k_ref, v_ref, g_ref = run
        rows, width = q_ref.shape
        wide = width // len(parts)
        factors = ((q_ref, before, PLAIN), (g_ref, before, LANES), (v_ref, after, LANES), (k_ref, after, PLAIN))
        block = min(rows, ACROSS_ROWS)
        for start in range(0, rows, block):
            here = pl.ds(start, block)
            for i, (factor, state, dims) in enumerate(factors):
                for h in range(width // DH):
                    at = h * DH
                    part = parts[at // wide][i][here, pl.ds(at % wide, DH)]
                    term = dot(factor[here, pl.ds(at, DH)], state[h], dims)
                    done_ref[n, i, here, pl.ds(at, DH)] = (part + term).astype(BF16)
                there = outs[i].at[here, pl.ds(first * DH, width)]
                moves.append(pltpu.make_async_copy(done_ref.at[n, i, here], there, sems.at[len(moves)]))
                moves[-1].start()
    token_ref[...] = jnp.zeros_like(token_ref)
    for move in moves:
        move.wait()


def across(jobs, outs, shape, size, after):
    held = () if outs is None else tuple(outs)
    arrays = [a for _, _, run, parts, sources in jobs for a in [*run, *sum(map(list, parts), []), *sources]]
    *outs, token = pl.pallas_call(
        functools.partial(
            across_kernel, [(total, first, len(parts), len(sources)) for total, first, _, parts, sources in jobs]
        ),
        in_specs=[VMEM] * len(arrays) + [HBM] * len(held) + [VMEM] * len(after),
        out_specs=[HBM] * 4 + [VMEM],
        out_shape=[jax.ShapeDtypeStruct(shape, BF16)] * 4 + [pltpu.VMEM((8, DH), F32)],
        input_output_aliases={len(arrays) + i: i for i in range(len(held))},
        scratch_shapes=[
            pltpu.VMEM((len(jobs), 4, shape[0], size * DH), BF16),
            pltpu.SemaphoreType.DMA((4 * len(jobs) * max(1, shape[0] // ACROSS_ROWS),)),
        ],
        compiler_params=PARAMS,
        cost_estimate=cost(1.5 * len(jobs)),
        name="across",
    )(*kept(arrays), *held, *kept(after))
    return outs, token


def body(*arrays):
    heads = arrays[0].shape[1] // DH
    runs, groups_of_heads = lax.axis_size("ctx"), lax.axis_size("seq")
    chain = runs // 2
    parts = 4
    size = heads // parts
    shape = (size, DH, DH)
    run = [[None] * 4 for _ in range(parts)]
    own = [None] * parts
    pieces = min(size, 2)
    local = [[None] * pieces for _ in range(parts)]
    swapped = {}
    got = {}
    last = []
    pair = [(r, r ^ 1) for r in range(runs)]

    def swap(parity):
        perm = []
        for r in range(runs):
            z, c = r // 2, r % 2
            mate = z + 1 if z % 2 == parity else z - 1
            for s in range(groups_of_heads):
                if 0 <= mate < chain:
                    to = (2 * mate + c) * groups_of_heads + s
                else:
                    to = r * groups_of_heads + (s ^ 1)
                perm.append((r * groups_of_heads + s, to))
        return perm

    def arrival(p, z, way):
        if way == 0:
            return None if z == 0 else ((z - 1) % 2, p + z - 1)
        return None if z == chain - 1 else (z % 2, p + chain - 2 - z)

    def bring(*chosen):
        found = load(arrays, [p * size for p in chosen], size, last)
        for n, p in enumerate(chosen):
            *run[p], own[p] = found[5 * n : 5 * n + 5]
        last[:] = [own[chosen[0]]]

    def inside(p, piece):
        wide = max(1, size // 2)
        local[p][piece] = within(run[p], piece * wide, wide * DH, last)
        last[:] = [local[p][piece][0]]

    def trade(p):
        if p >= 2:
            swapped[p] = lax.ppermute(own[p], "ctx", pair)
            return
        keys = sorted({arrival(p, z, way) for z in range(chain) for way in range(2)} - {None})

        def function(row, column, refs, out):
            for way, near in ((0, 0), (1, 1)):
                value = jnp.where(column == near, refs[0][way], 0.0)
                out[way] = value + chained(p, way, row, refs[1:], keys)

        payload = mix(function, (2,) + shape, [own[p]] + [got[k] for k in keys], last, "trade")
        last[:] = [payload]
        swapped[p] = lax.ppermute(payload, "ctx", pair)

    def chained(p, way, row, refs, keys):
        total = jnp.zeros(shape, F32)
        for key, ref in zip(keys, refs, strict=True):
            places = [z for z in range(chain) if arrival(p, z, way) == key]
            if places:
                total = jnp.where(any_of(row, places), ref[...], total)
        return total

    def hop(parity, slot):
        groups = {}
        for link in range(parity, chain - 1, 2):
            for way, p, z in ((0, slot - link, link), (1, slot - (chain - 2 - link), link + 1)):
                if 0 <= p < parts:
                    groups.setdefault((p, arrival(p, z, way)), ([], []))[way].append(z)
        if not groups:
            return
        names = []

        def use(name):
            if name not in names:
                names.append(name)

        for p, key in groups:
            use(("own", p))
            if p >= 2:
                use(("swapped", p))
            if key is not None:
                use(("got", key))
        tables = {"own": own, "swapped": swapped, "got": got}
        values = [tables[kind][key] for kind, key in names]

        def function(row, column, refs, out):
            refs = dict(zip(names, refs, strict=True))
            payload = None
            for (p, key), (up, down) in groups.items():
                def state(way):
                    value = refs["own", p][way]
                    return value + refs["swapped", p][way] if p >= 2 else value

                if up and down:
                    value = jnp.where(any_of(row, up), state(0), state(1))
                else:
                    value = state(0 if up else 1)
                if key is not None:
                    value = value + refs["got", key][...]
                payload = value if payload is None else jnp.where(any_of(row, up + down), value, payload)
            out[...] = payload

        payload = mix(function, shape, values, last, "hop")
        last[:] = [payload]
        got[parity, slot] = lax.ppermute(payload, ("ctx", "seq"), swap(parity))

    outs = [None]

    def finish(*chosen):
        jobs = []
        for p in chosen:
            keys = sorted({arrival(p, z, way) for z in range(chain) for way in range(2)} - {None})

            def total(row, column, refs, p=p, keys=keys):
                for way, far in ((0, 1), (1, 0)):
                    value = refs[0][way]
                    if p >= 2:
                        value = jnp.where(column == far, value, 0.0)
                    yield value + chained(p, way, row, refs[1:], keys)

            jobs.append((total, p * size, run[p], local[p], [swapped[p]] + [got[k] for k in keys]))
        outs[0], token = across(jobs, outs[0], arrays[0].shape, size, last)
        last[:] = [token]

    steps = {"L": bring, "X": trade, "E": functools.partial(hop, 0), "O": functools.partial(hop, 1), "W": inside, "A": finish}
    order = [(name[0], [int(n) for n in name[1:]]) for name in ORDER]
    if chain != 4:
        order = [("L", [2, 0]), ("X", [2]), ("L", [1, 3]), ("X", [3])]
        order += [("W", [p, n]) for p in range(parts) for n in range(pieces)]
        order += [(kind, [t]) for t in range(parts + chain - 2) for kind in "EO"]
        order += [("X", [0]), ("X", [1]), ("A", [2, 3]), ("A", [0, 1])]
    for kind, numbers in order:
        steps[kind](*numbers)
    return tuple(outs[0])


def solution(mesh):
    spec = P("ctx", "seq")
    return jax.shard_map(body, mesh=mesh, in_specs=(spec,) * 4, out_specs=(spec,) * 4, check_vma=False)
```

```python
import functools

import jax
import jax.numpy as jnp
from jax import lax
from jax.experimental import pallas as pl
from jax.experimental.pallas import tpu as pltpu
from jax.sharding import PartitionSpec as P

DH = 128
F32 = jnp.float32
BF16 = jnp.bfloat16
ROWS = ((0,), (0,))
LANES = ((1,), (1,))
PLAIN = ((1,), (0,))
VMEM = pl.BlockSpec(memory_space=pltpu.VMEM)
HBM = pl.BlockSpec(memory_space=pltpu.HBM)
ACROSS_ROWS = 256
ORDER = (
    "L023", "E0", "S0", "L1", "E1", "W20", "O1", "S1", "W21", "W00", "E2", "O2", "W01", "W10",
    "E3", "O3", "X0", "W11", "O4", "E4", "X1", "W30", "W31", "E5", "A0", "A2", "A31",
)
PARAMS = pltpu.CompilerParams(vmem_limit_bytes=8 << 20)


def cost(us):
    return pl.CostEstimate(flops=int(us * 1.15e9), transcendentals=0, bytes_accessed=1)


def dot(a, b, dims):
    return lax.dot_general(a, b, (dims, ((), ())), preferred_element_type=F32)


def kept(arrays):
    return [pltpu.with_memory_space_constraint(a, pltpu.VMEM) for a in arrays]


def any_of(place, places):
    return functools.reduce(jnp.logical_or, [place == p for p in places])


def spot():
    place = lax.axis_index("ctx")
    return place // 2, place % 2


def load_kernel(firsts, q_hbm, k_hbm, v_hbm, g_hbm, *refs):
    *refs, sems = refs
    parts = [refs[len(refs) - 5 * (len(firsts) - n) :][:5] for n in range(len(firsts))]
    moves = []
    for n, (first, part) in enumerate(zip(firsts, parts, strict=True)):
        there = pl.ds(first * DH, part[0].shape[1])
        pairs = ((k_hbm, part[1]), (v_hbm, part[2]), (q_hbm, part[0]), (g_hbm, part[3]))
        moves.append([pltpu.make_async_copy(src.at[:, there], dst, sems.at[n, i]) for i, (src, dst) in enumerate(pairs)])
        for move in moves[-1]:
            move.start()
    for part, own in zip(parts, moves, strict=True):
        q_ref, k_ref, v_ref, g_ref, state_ref = part
        size = state_ref.shape[1]
        cols = [slice(h * DH, (h + 1) * DH) for h in range(size)]
        own[0].wait()
        own[1].wait()
        for h in range(size):
            state_ref[0, h] = dot(k_ref[:, cols[h]], v_ref[:, cols[h]], ROWS)
        own[2].wait()
        own[3].wait()
        for h in range(size):
            state_ref[1, h] = dot(q_ref[:, cols[h]], g_ref[:, cols[h]], ROWS)


def load(arrays, firsts, size, after):
    rows = arrays[0].shape[0]
    part = [pltpu.VMEM((rows, size * DH), BF16)] * 4 + [pltpu.VMEM((2, size, DH, DH), F32)]
    return pl.pallas_call(
        functools.partial(load_kernel, firsts),
        in_specs=[HBM] * 4 + [VMEM] * len(after),
        out_specs=[VMEM] * (5 * len(firsts)),
        out_shape=part * len(firsts),
        scratch_shapes=[pltpu.SemaphoreType.DMA((len(firsts), 4))],
        compiler_params=PARAMS,
        cost_estimate=cost(1.5 + 0.5 * len(firsts)),
        name="load",
    )(*[pltpu.with_memory_space_constraint(a, pltpu.HBM) for a in arrays], *kept(after))


def within_kernel(tile, first, *refs):
    q_ref, k_ref, v_ref, g_ref = refs[:4]
    attended_ref, query_ref, key_ref, value_ref = refs[-4:]
    rows, width = attended_ref.shape
    count = rows // tile
    causal = lax.broadcasted_iota(jnp.int32, (tile, tile), 1) <= lax.broadcasted_iota(jnp.int32, (tile, tile), 0)

    @pl.loop(0, width // DH)
    def _(h):
        lanes, source = (pl.ds(pl.multiple_of(n * DH, DH), DH) for n in (h, first + h))
        at = [pl.ds(i * tile, tile) for i in range(count)]
        q, k, v, g = ([ref[a, source] for a in at] for ref in (q_ref, k_ref, v_ref, g_ref))
        attn, grads = {}, {}
        for i in range(count):
            for j in range(i + 1):
                a, b = dot(q[i], k[j], LANES), dot(g[i], v[j], LANES)
                if i == j:
                    a, b = jnp.where(causal, a, 0.0), jnp.where(causal, b, 0.0)
                attn[i, j], grads[i, j] = a.astype(BF16), b.astype(BF16)
        for i in range(count):
            attended_ref[at[i], lanes] = sum(dot(attn[i, j], v[j], PLAIN) for j in range(i + 1))
            query_ref[at[i], lanes] = sum(dot(grads[i, j], k[j], PLAIN) for j in range(i + 1))
        for j in range(count):
            key_ref[at[j], lanes] = sum(dot(grads[i, j], q[i], ROWS) for i in range(j, count))
            value_ref[at[j], lanes] = sum(dot(attn[i, j], g[i], ROWS) for i in range(j, count))


def within(run, first, width, after):
    rows = run[0].shape[0]
    return pl.pallas_call(
        functools.partial(within_kernel, min(rows, 256), first),
        in_specs=[VMEM] * (4 + len(after)),
        out_specs=[VMEM] * 4,
        out_shape=[pltpu.VMEM((rows, width), F32)] * 4,
        compiler_params=PARAMS,
        cost_estimate=cost(1.5),
        name="within",
    )(*kept(run), *kept(after))


def mix(function, shape, arrays, after, name):
    def kernel(*refs):
        row, column = spot()
        function(row, column, refs[: len(arrays)], refs[-1])

    return pl.pallas_call(
        kernel,
        in_specs=[VMEM] * (len(arrays) + len(after)),
        out_specs=VMEM,
        out_shape=pltpu.VMEM(shape, F32),
        compiler_params=PARAMS,
        cost_estimate=cost(3),
        name=name,
    )(*kept(arrays), *kept(after))


def across_kernel(jobs, *refs):
    *outs, token_ref, done_ref, sems = refs[-7:]
    row, column = spot()
    moves, ready = [], []
    for total, first, pieces, count in jobs:
        run, refs = refs[:4], refs[4:]
        parts, refs = [refs[4 * n : 4 * n + 4] for n in range(pieces)], refs[4 * pieces :]
        sources, refs = refs[:count], refs[count:]
        ready.append((run, parts, first, [value.astype(BF16) for value in total(row, column, sources)]))
    for n, (run, parts, first, (before, after)) in enumerate(ready):
        q_ref, k_ref, v_ref, g_ref = run
        rows, width = q_ref.shape
        wide = width // len(parts)
        factors = ((q_ref, before, PLAIN), (g_ref, before, LANES), (v_ref, after, LANES), (k_ref, after, PLAIN))
        block = min(rows, ACROSS_ROWS)
        for start in range(0, rows, block):
            here = pl.ds(start, block)
            for i, (factor, state, dims) in enumerate(factors):
                for h in range(width // DH):
                    at = h * DH
                    part = parts[at // wide][i][here, pl.ds(at % wide, DH)]
                    term = dot(factor[here, pl.ds(at, DH)], state[h], dims)
                    done_ref[n, i, here, pl.ds(at, DH)] = (part + term).astype(BF16)
                there = outs[i].at[here, pl.ds(first * DH, width)]
                moves.append(pltpu.make_async_copy(done_ref.at[n, i, here], there, sems.at[len(moves)]))
                moves[-1].start()
    token_ref[...] = jnp.zeros_like(token_ref)
    for move in moves:
        move.wait()


def across(jobs, outs, shape, size, after):
    held = () if outs is None else tuple(outs)
    arrays = [a for _, _, run, parts, sources in jobs for a in [*run, *sum(map(list, parts), []), *sources]]
    *outs, token = pl.pallas_call(
        functools.partial(
            across_kernel, [(total, first, len(parts), len(sources)) for total, first, _, parts, sources in jobs]
        ),
        in_specs=[VMEM] * len(arrays) + [HBM] * len(held) + [VMEM] * len(after),
        out_specs=[HBM] * 4 + [VMEM],
        out_shape=[jax.ShapeDtypeStruct(shape, BF16)] * 4 + [pltpu.VMEM((8, DH), F32)],
        input_output_aliases={len(arrays) + i: i for i in range(len(held))},
        scratch_shapes=[
            pltpu.VMEM((len(jobs), 4, shape[0], size * DH), BF16),
            pltpu.SemaphoreType.DMA((4 * len(jobs) * max(1, shape[0] // ACROSS_ROWS),)),
        ],
        compiler_params=PARAMS,
        cost_estimate=cost(1.5 * len(jobs)),
        name="across",
    )(*kept(arrays), *held, *kept(after))
    return outs, token


def body(*arrays):
    heads = arrays[0].shape[1] // DH
    runs, groups_of_heads = lax.axis_size("ctx"), lax.axis_size("seq")
    chain = runs // 2
    relay = chain == 4
    parts = 4
    size = heads // parts
    shape = (size, DH, DH)
    run = [[None] * 4 for _ in range(parts)]
    own = [None] * parts
    pieces = min(size, 2)
    local = [[None] * pieces for _ in range(parts)]
    got, turns, swapped = {}, {}, {}
    last = []
    pair = [(r, r ^ 1) for r in range(runs)]

    def early(row):
        return row < chain // 2

    def near(row, column):
        return ((row == 0) & (column == 0)) | ((row == chain - 1) & (column == 1))

    def end(row):
        return (row == 0) | (row == chain - 1)

    def far(row, column):
        return end(row) & jnp.logical_not(near(row, column))

    def swap(parity):
        perm = []
        for r in range(runs):
            z, c = r // 2, r % 2
            mate = z + 1 if z % 2 == parity else z - 1
            for s in range(groups_of_heads):
                if 0 <= mate < chain:
                    to = (2 * mate + c) * groups_of_heads + s
                else:
                    to = r * groups_of_heads + (s ^ 1)
                perm.append((r * groups_of_heads + s, to))
        return perm

    def arrival(p, z, way):
        if way == 0:
            return None if z == 0 else ((z - 1) % 2, p + z - 1)
        return None if z == chain - 1 else (z % 2, p + chain - 2 - z)

    def bring(*chosen):
        found = load(arrays, [p * size for p in chosen], size, last)
        for n, p in enumerate(chosen):
            *run[p], own[p] = found[5 * n : 5 * n + 5]
        last[:] = [own[chosen[0]]]

    def inside(p, piece):
        wide = max(1, size // 2)
        local[p][piece] = within(run[p], piece * wide, wide * DH, last)
        last[:] = [local[p][piece][0]]

    def share(turn):
        values = [own[2], own[3]]
        if turn and relay:
            values += [own[0], got[0, 0]]

        def function(row, column, refs, out):
            for n in range(2):
                first, then = refs[n][0], refs[n][1]
                value = jnp.where(early(row), *((then, first) if turn else (first, then)))
                if turn and relay:
                    mine = jnp.where(early(row), refs[2][0], refs[2][1])
                    value = jnp.where(near(row, column), mine + refs[3][...] if n else mine, value)
                    if n:
                        value = jnp.where(far(row, column), mine, value)
                out[n] = value

        payload = mix(function, (2,) + shape, values, last, "share")
        last[:] = [payload]
        turns[turn] = lax.ppermute(payload, "ctx", pair)

    def trade(p):
        keys = sorted({arrival(p, z, way) for z in range(chain) for way in range(2)} - {None})
        small = relay and p == 0
        values = [own[p]] + [got[k] for k in keys] + ([own[3]] if relay and p == 1 else [])

        def function(row, column, refs, out):
            sums = []
            for way in range(2):
                value = jnp.where(column == way, refs[0][way], 0.0) + chained(p, way, row, refs[1:], keys)
                if relay and p == 1:
                    late = (row == (0, chain - 1)[way]) & (column == 1 - way)
                    value = jnp.where(late, refs[-1][1 - way], value)
                sums.append(value)
            if small:
                out[...] = jnp.where(early(row), sums[1], sums[0])
            else:
                out[0], out[1] = sums

        payload = mix(function, shape if small else (2,) + shape, values, last, "trade")
        last[:] = [payload]
        swapped[p] = lax.ppermute(payload, "ctx", pair)

    def chained(p, way, row, refs, keys):
        total = jnp.zeros(shape, F32)
        for key, ref in zip(keys, refs):
            places = [z for z in range(chain) if arrival(p, z, way) == key]
            if places:
                total = jnp.where(any_of(row, places), ref[...], total)
        return total

    def hop(parity, slot):
        groups = {}
        for link in range(parity, chain - 1, 2):
            for way, p, z in ((0, slot - link, link), (1, slot - (chain - 2 - link), link + 1)):
                if 0 <= p < parts:
                    groups.setdefault((p, arrival(p, z, way)), ([], []))[way].append(z)
        if not groups:
            return
        def turn_of(way, z):
            return 0 if early(z) == (way == 0) else 1

        forward = relay and parity == 0 and slot == 4
        names = []
        for (p, key), ways in groups.items():
            names.append(("own", p))
            if p >= 2:
                names += [("turns", turn_of(way, z)) for way in range(2) for z in ways[way]]
            if key is not None:
                names.append(("got", key))
        if forward:
            names.append(("turns", 1))
        names = list(dict.fromkeys(names))
        tables = {"own": own, "turns": turns, "got": got}
        values = [tables[kind][key] for kind, key in names]

        def function(row, column, refs, out):
            refs = dict(zip(names, refs, strict=True))

            def state(p, way, rows):
                value = refs["own", p][way]
                if p >= 2:
                    found = {turn_of(way, z) for z in rows}
                    ways = [refs["turns", turn][p - 2] if turn in found else None for turn in range(2)]
                    if len(found) == 2:
                        other = jnp.where(early(row) == (way == 0), *ways)
                    else:
                        other = ways[found.pop()]
                    value = value + other
                return value

            payload = None
            for (p, key), (up, down) in groups.items():
                if up and down:
                    rising = early(row) if relay and slot == 0 else any_of(row, up)
                    value = jnp.where(rising, state(p, 0, up), state(p, 1, down))
                else:
                    value = state(p, 0, up) if up else state(p, 1, down)
                if key is not None:
                    value = value + refs["got", key][...]
                payload = value if payload is None else jnp.where(any_of(row, up + down), value, payload)
            if forward:
                payload = jnp.where(end(row), refs["turns", 1][1], payload)
            out[...] = payload

        payload = mix(function, shape, values, last, "hop")
        last[:] = [payload]
        got[parity, slot] = lax.ppermute(payload, ("ctx", "seq"), swap(parity))

    outs = [None]

    def finish(*chosen):
        jobs = []
        for p in chosen:
            keys = sorted({arrival(p, z, way) for z in range(chain) for way in range(2)} - {None})

            values = {("got", k): got[k] for k in keys}
            if p >= 2:
                values |= {("turns", n): turns[n] for n in range(2)}
            else:
                values["swapped", p] = swapped[p]
            if relay and p == 3:
                values["swapped", 1] = swapped[1]
            if relay and p == 0:
                values |= {("turns", 1): turns[1], ("got", (0, 4)): got[0, 4]}

            def total(row, column, refs, p=p, keys=keys, names=tuple(values)):
                refs = dict(zip(names, refs, strict=True))
                for way in range(2):
                    head, tail = (0, chain - 1) if way == 0 else (chain - 1, 0)
                    if p >= 2:
                        extra = jnp.where(early(row) == (way == 0), refs["turns", 0][p - 2], refs["turns", 1][p - 2])
                        if relay and p == 3:
                            extra = jnp.where(row == tail, refs["swapped", 1][1 - way], extra)
                        extra = jnp.where(column == 1 - way, extra, 0.0)
                    elif relay and p == 0:
                        extra = jnp.where(early(row) == (way == 0), refs["got", (0, 4)][...], refs["swapped", 0][...])
                        extra = jnp.where(row == head, refs["turns", 1][0], extra)
                    else:
                        extra = refs["swapped", p][way]
                    if p < 2:
                        extra = jnp.where((row == head) & (column == way), 0.0, extra)
                    yield extra + chained(p, way, row, [refs["got", k] for k in keys], keys)

            jobs.append((total, p * size, run[p], local[p], list(values.values())))
        outs[0], token = across(jobs, outs[0], arrays[0].shape, size, last)
        last[:] = [token]

    steps = {"L": bring, "S": share, "X": trade, "E": functools.partial(hop, 0), "O": functools.partial(hop, 1), "W": inside, "A": finish}
    order = [(name[0], [int(n) for n in name[1:]]) for name in ORDER]
    if chain != 4:
        order = [("L", [2, 3]), ("L", [0, 1]), ("S", [0]), ("S", [1])]
        order += [("W", [p, n]) for p in range(parts) for n in range(pieces)]
        order += [(kind, [t]) for t in range(parts + chain - 2) for kind in "EO"]
        order += [("X", [0]), ("X", [1]), ("A", [2, 3]), ("A", [0, 1])]
    for kind, numbers in order:
        steps[kind](*numbers)
    return tuple(outs[0])


def solution(mesh):
    spec = P("ctx", "seq")
    return jax.shard_map(body, mesh=mesh, in_specs=(spec,) * 4, out_specs=(spec,) * 4, check_vma=False)
```

```python
import functools

import jax
import jax.numpy as jnp
from jax import lax
from jax.experimental import pallas as pl
from jax.experimental.pallas import tpu as pltpu
from jax.sharding import PartitionSpec as P

DH = 128
F32 = jnp.float32
BF16 = jnp.bfloat16
ROWS = ((0,), (0,))
LANES = ((1,), (1,))
PLAIN = ((1,), (0,))
VMEM = pl.BlockSpec(memory_space=pltpu.VMEM)
HBM = pl.BlockSpec(memory_space=pltpu.HBM)
ACROSS_ROWS = 256
ORDER = (
    "F", "E0", "S0", "L0123", "E1", "O1", "W20", "S1", "W21", "O2", "E2", "W00", "W01", "W10",
    "E3", "O3", "X0", "W11", "O4", "E4", "X1", "W30", "W31", "E5", "A0", "A2", "A31",
)
PARAMS = pltpu.CompilerParams(vmem_limit_bytes=8 << 20)


def cost(us):
    return pl.CostEstimate(flops=int(us * 1.15e9), transcendentals=0, bytes_accessed=1)


def dot(a, b, dims):
    return lax.dot_general(a, b, (dims, ((), ())), preferred_element_type=F32)


def kept(arrays):
    return [pltpu.with_memory_space_constraint(a, pltpu.VMEM) for a in arrays]


def any_of(place, places):
    return functools.reduce(jnp.logical_or, [place == p for p in places])


def spot():
    place = lax.axis_index("ctx")
    return place // 2, place % 2


def first_kernel(firsts, chain, q_hbm, k_hbm, v_hbm, g_hbm, opening_ref, shared_ref, a_ref, b_ref, sems):
    row, _ = spot()
    size = opening_ref.shape[0]
    upper = row < chain // 2

    def moves(a_hbm, b_hbm):
        for n, first in enumerate(firsts):
            there = pl.ds(first * DH, size * DH)
            yield pltpu.make_async_copy(a_hbm.at[:, there], a_ref.at[n], sems.at[n, 0])
            yield pltpu.make_async_copy(b_hbm.at[:, there], b_ref.at[n], sems.at[n, 1])

    @pl.when(upper)
    def _():
        for move in moves(k_hbm, v_hbm):
            move.start()

    @pl.when(jnp.logical_not(upper))
    def _():
        for move in moves(q_hbm, g_hbm):
            move.start()

    waits = list(moves(k_hbm, v_hbm))
    for n, out in enumerate((opening_ref, shared_ref.at[0], shared_ref.at[1])):
        waits[2 * n].wait()
        waits[2 * n + 1].wait()
        for h in range(size):
            cols = slice(h * DH, (h + 1) * DH)
            out[h] = dot(a_ref[n, :, cols], b_ref[n, :, cols], ROWS)


def first_states(arrays, firsts, size, chain):
    block = (3, arrays[0].shape[0], size * DH)
    return pl.pallas_call(
        functools.partial(first_kernel, firsts, chain),
        in_specs=[HBM] * 4,
        out_specs=[VMEM] * 2,
        out_shape=[pltpu.VMEM((size, DH, DH), F32), pltpu.VMEM((2, size, DH, DH), F32)],
        scratch_shapes=[pltpu.VMEM(block, BF16), pltpu.VMEM(block, BF16), pltpu.SemaphoreType.DMA((3, 2))],
        compiler_params=PARAMS,
        cost_estimate=cost(2.5),
        name="first",
    )(*[pltpu.with_memory_space_constraint(a, pltpu.HBM) for a in arrays])


def load_kernel(firsts, q_hbm, k_hbm, v_hbm, g_hbm, *refs):
    *refs, sems = refs
    parts = [refs[len(refs) - 5 * (len(firsts) - n) :][:5] for n in range(len(firsts))]
    moves = []
    for n, (first, part) in enumerate(zip(firsts, parts, strict=True)):
        there = pl.ds(first * DH, part[0].shape[1])
        pairs = ((k_hbm, part[1]), (v_hbm, part[2]), (q_hbm, part[0]), (g_hbm, part[3]))
        moves.append([pltpu.make_async_copy(src.at[:, there], dst, sems.at[n, i]) for i, (src, dst) in enumerate(pairs)])
        for move in moves[-1]:
            move.start()
    for part, own in zip(parts, moves, strict=True):
        q_ref, k_ref, v_ref, g_ref, state_ref = part
        size = state_ref.shape[1]
        cols = [slice(h * DH, (h + 1) * DH) for h in range(size)]
        own[0].wait()
        own[1].wait()
        for h in range(size):
            state_ref[0, h] = dot(k_ref[:, cols[h]], v_ref[:, cols[h]], ROWS)
        own[2].wait()
        own[3].wait()
        for h in range(size):
            state_ref[1, h] = dot(q_ref[:, cols[h]], g_ref[:, cols[h]], ROWS)


def load(arrays, firsts, size, after):
    rows = arrays[0].shape[0]
    part = [pltpu.VMEM((rows, size * DH), BF16)] * 4 + [pltpu.VMEM((2, size, DH, DH), F32)]
    return pl.pallas_call(
        functools.partial(load_kernel, firsts),
        in_specs=[HBM] * 4 + [VMEM] * len(after),
        out_specs=[VMEM] * (5 * len(firsts)),
        out_shape=part * len(firsts),
        scratch_shapes=[pltpu.SemaphoreType.DMA((len(firsts), 4))],
        compiler_params=PARAMS,
        cost_estimate=cost(1.5 + 0.5 * len(firsts)),
        name="load",
    )(*[pltpu.with_memory_space_constraint(a, pltpu.HBM) for a in arrays], *kept(after))


def within_kernel(tile, first, *refs):
    q_ref, k_ref, v_ref, g_ref = refs[:4]
    attended_ref, query_ref, key_ref, value_ref = refs[-4:]
    rows, width = attended_ref.shape
    count = rows // tile
    causal = lax.broadcasted_iota(jnp.int32, (tile, tile), 1) <= lax.broadcasted_iota(jnp.int32, (tile, tile), 0)

    @pl.loop(0, width // DH)
    def _(h):
        lanes, source = (pl.ds(pl.multiple_of(n * DH, DH), DH) for n in (h, first + h))
        at = [pl.ds(i * tile, tile) for i in range(count)]
        q, k, v, g = ([ref[a, source] for a in at] for ref in (q_ref, k_ref, v_ref, g_ref))
        attn, grads = {}, {}
        for i in range(count):
            for j in range(i + 1):
                a, b = dot(q[i], k[j], LANES), dot(g[i], v[j], LANES)
                if i == j:
                    a, b = jnp.where(causal, a, 0.0), jnp.where(causal, b, 0.0)
                attn[i, j], grads[i, j] = a.astype(BF16), b.astype(BF16)
        for i in range(count):
            attended_ref[at[i], lanes] = sum(dot(attn[i, j], v[j], PLAIN) for j in range(i + 1))
            query_ref[at[i], lanes] = sum(dot(grads[i, j], k[j], PLAIN) for j in range(i + 1))
        for j in range(count):
            key_ref[at[j], lanes] = sum(dot(grads[i, j], q[i], ROWS) for i in range(j, count))
            value_ref[at[j], lanes] = sum(dot(attn[i, j], g[i], ROWS) for i in range(j, count))


def within(run, first, width, after):
    rows = run[0].shape[0]
    return pl.pallas_call(
        functools.partial(within_kernel, min(rows, 256), first),
        in_specs=[VMEM] * (4 + len(after)),
        out_specs=[VMEM] * 4,
        out_shape=[pltpu.VMEM((rows, width), F32)] * 4,
        compiler_params=PARAMS,
        cost_estimate=cost(1.5),
        name="within",
    )(*kept(run), *kept(after))


def mix(function, shape, arrays, after, name):
    def kernel(*refs):
        row, column = spot()
        function(row, column, refs[: len(arrays)], refs[-1])

    return pl.pallas_call(
        kernel,
        in_specs=[VMEM] * (len(arrays) + len(after)),
        out_specs=VMEM,
        out_shape=pltpu.VMEM(shape, F32),
        compiler_params=PARAMS,
        cost_estimate=cost(3),
        name=name,
    )(*kept(arrays), *kept(after))


def across_kernel(jobs, *refs):
    *outs, token_ref, done_ref, sems = refs[-7:]
    row, column = spot()
    moves, ready = [], []
    for total, first, pieces, count in jobs:
        run, refs = refs[:4], refs[4:]
        parts, refs = [refs[4 * n : 4 * n + 4] for n in range(pieces)], refs[4 * pieces :]
        sources, refs = refs[:count], refs[count:]
        ready.append((run, parts, first, [value.astype(BF16) for value in total(row, column, sources)]))
    for n, (run, parts, first, (before, after)) in enumerate(ready):
        q_ref, k_ref, v_ref, g_ref = run
        rows, width = q_ref.shape
        wide = width // len(parts)
        factors = ((q_ref, before, PLAIN), (g_ref, before, LANES), (v_ref, after, LANES), (k_ref, after, PLAIN))
        block = min(rows, ACROSS_ROWS)
        for start in range(0, rows, block):
            here = pl.ds(start, block)
            for i, (factor, state, dims) in enumerate(factors):
                for h in range(width // DH):
                    at = h * DH
                    part = parts[at // wide][i][here, pl.ds(at % wide, DH)]
                    term = dot(factor[here, pl.ds(at, DH)], state[h], dims)
                    done_ref[n, i, here, pl.ds(at, DH)] = (part + term).astype(BF16)
                there = outs[i].at[here, pl.ds(first * DH, width)]
                moves.append(pltpu.make_async_copy(done_ref.at[n, i, here], there, sems.at[len(moves)]))
                moves[-1].start()
    token_ref[...] = jnp.zeros_like(token_ref)
    for move in moves:
        move.wait()


def across(jobs, outs, shape, size, after):
    held = () if outs is None else tuple(outs)
    arrays = [a for _, _, run, parts, sources in jobs for a in [*run, *sum(map(list, parts), []), *sources]]
    *outs, token = pl.pallas_call(
        functools.partial(
            across_kernel, [(total, first, len(parts), len(sources)) for total, first, _, parts, sources in jobs]
        ),
        in_specs=[VMEM] * len(arrays) + [HBM] * len(held) + [VMEM] * len(after),
        out_specs=[HBM] * 4 + [VMEM],
        out_shape=[jax.ShapeDtypeStruct(shape, BF16)] * 4 + [pltpu.VMEM((8, DH), F32)],
        input_output_aliases={len(arrays) + i: i for i in range(len(held))},
        scratch_shapes=[
            pltpu.VMEM((len(jobs), 4, shape[0], size * DH), BF16),
            pltpu.SemaphoreType.DMA((4 * len(jobs) * max(1, shape[0] // ACROSS_ROWS),)),
        ],
        compiler_params=PARAMS,
        cost_estimate=cost(1.5 * len(jobs)),
        name="across",
    )(*kept(arrays), *held, *kept(after))
    return outs, token


def body(*arrays):
    heads = arrays[0].shape[1] // DH
    runs, groups_of_heads = lax.axis_size("ctx"), lax.axis_size("seq")
    chain = runs // 2
    relay = chain == 4
    parts = 4
    size = heads // parts
    shape = (size, DH, DH)
    run = [[None] * 4 for _ in range(parts)]
    own = [None] * parts
    pieces = min(size, 2)
    local = [[None] * pieces for _ in range(parts)]
    got, turns, swapped = {}, {}, {}
    last, opening = [], []
    pair = [(r, r ^ 1) for r in range(runs)]

    def early(row):
        return row < chain // 2

    def near(row, column):
        return ((row == 0) & (column == 0)) | ((row == chain - 1) & (column == 1))

    def end(row):
        return (row == 0) | (row == chain - 1)

    def far(row, column):
        return end(row) & jnp.logical_not(near(row, column))

    def swap(parity):
        perm = []
        for r in range(runs):
            z, c = r // 2, r % 2
            mate = z + 1 if z % 2 == parity else z - 1
            for s in range(groups_of_heads):
                if 0 <= mate < chain:
                    to = (2 * mate + c) * groups_of_heads + s
                else:
                    to = r * groups_of_heads + (s ^ 1)
                perm.append((r * groups_of_heads + s, to))
        return perm

    def arrival(p, z, way):
        if way == 0:
            return None if z == 0 else ((z - 1) % 2, p + z - 1)
        return None if z == chain - 1 else (z % 2, p + chain - 2 - z)

    def bring(*chosen):
        found = load(arrays, [p * size for p in chosen], size, last)
        for n, p in enumerate(chosen):
            *run[p], own[p] = found[5 * n : 5 * n + 5]
        last[:] = [own[chosen[0]]]

    def begin():
        opening[:] = first_states(arrays, [p * size for p in (0, 2, 3)], size, chain)
        last[:] = [opening[0]]

    def inside(p, piece):
        wide = max(1, size // 2)
        local[p][piece] = within(run[p], piece * wide, wide * DH, last)
        last[:] = [local[p][piece][0]]

    def share(turn):
        if opening and not turn:
            turns[0] = lax.ppermute(opening[1], "ctx", pair)
            return
        values = [own[2], own[3]]
        if turn and relay:
            values += [own[0], got[0, 0]]

        def function(row, column, refs, out):
            for n in range(2):
                first, then = refs[n][0], refs[n][1]
                value = jnp.where(early(row), *((then, first) if turn else (first, then)))
                if turn and relay:
                    mine = jnp.where(early(row), refs[2][0], refs[2][1])
                    value = jnp.where(near(row, column), mine + refs[3][...] if n else mine, value)
                    if n:
                        value = jnp.where(far(row, column), mine, value)
                out[n] = value

        payload = mix(function, (2,) + shape, values, last, "share")
        last[:] = [payload]
        turns[turn] = lax.ppermute(payload, "ctx", pair)

    def trade(p):
        keys = sorted({arrival(p, z, way) for z in range(chain) for way in range(2)} - {None})
        small = relay and p == 0
        values = [own[p]] + [got[k] for k in keys] + ([own[3]] if relay and p == 1 else [])

        def function(row, column, refs, out):
            sums = []
            for way in range(2):
                value = jnp.where(column == way, refs[0][way], 0.0) + chained(p, way, row, refs[1:], keys)
                if relay and p == 1:
                    late = (row == (0, chain - 1)[way]) & (column == 1 - way)
                    value = jnp.where(late, refs[-1][1 - way], value)
                sums.append(value)
            if small:
                out[...] = jnp.where(early(row), sums[1], sums[0])
            else:
                out[0], out[1] = sums

        payload = mix(function, shape if small else (2,) + shape, values, last, "trade")
        last[:] = [payload]
        swapped[p] = lax.ppermute(payload, "ctx", pair)

    def chained(p, way, row, refs, keys):
        total = jnp.zeros(shape, F32)
        for key, ref in zip(keys, refs):
            places = [z for z in range(chain) if arrival(p, z, way) == key]
            if places:
                total = jnp.where(any_of(row, places), ref[...], total)
        return total

    def hop(parity, slot):
        groups = {}
        for link in range(parity, chain - 1, 2):
            for way, p, z in ((0, slot - link, link), (1, slot - (chain - 2 - link), link + 1)):
                if 0 <= p < parts:
                    groups.setdefault((p, arrival(p, z, way)), ([], []))[way].append(z)
        if not groups:
            return
        def turn_of(way, z):
            return 0 if early(z) == (way == 0) else 1

        forward = relay and parity == 0 and slot == 4
        names = []
        for (p, key), ways in groups.items():
            names.append(("own", p))
            if p >= 2:
                names += [("turns", turn_of(way, z)) for way in range(2) for z in ways[way]]
            if key is not None:
                names.append(("got", key))
        if forward:
            names.append(("turns", 1))
        names = list(dict.fromkeys(names))
        tables = {"own": own, "turns": turns, "got": got}
        values = [tables[kind][key] for kind, key in names]

        def function(row, column, refs, out):
            refs = dict(zip(names, refs, strict=True))

            def state(p, way, rows):
                value = refs["own", p][way]
                if p >= 2:
                    found = {turn_of(way, z) for z in rows}
                    ways = [refs["turns", turn][p - 2] if turn in found else None for turn in range(2)]
                    if len(found) == 2:
                        other = jnp.where(early(row) == (way == 0), *ways)
                    else:
                        other = ways[found.pop()]
                    value = value + other
                return value

            payload = None
            for (p, key), (up, down) in groups.items():
                if up and down:
                    rising = early(row) if relay and slot == 0 else any_of(row, up)
                    value = jnp.where(rising, state(p, 0, up), state(p, 1, down))
                else:
                    value = state(p, 0, up) if up else state(p, 1, down)
                if key is not None:
                    value = value + refs["got", key][...]
                payload = value if payload is None else jnp.where(any_of(row, up + down), value, payload)
            if forward:
                payload = jnp.where(end(row), refs["turns", 1][1], payload)
            out[...] = payload

        if opening and (parity, slot) == (0, 0):
            payload = opening[0]
        else:
            payload = mix(function, shape, values, last, "hop")
            last[:] = [payload]
        got[parity, slot] = lax.ppermute(payload, ("ctx", "seq"), swap(parity))

    outs = [None]

    def finish(*chosen):
        jobs = []
        for p in chosen:
            keys = sorted({arrival(p, z, way) for z in range(chain) for way in range(2)} - {None})

            values = {("got", k): got[k] for k in keys}
            if p >= 2:
                values |= {("turns", n): turns[n] for n in range(2)}
            else:
                values["swapped", p] = swapped[p]
            if relay and p == 3:
                values["swapped", 1] = swapped[1]
            if relay and p == 0:
                values |= {("turns", 1): turns[1], ("got", (0, 4)): got[0, 4]}

            def total(row, column, refs, p=p, keys=keys, names=tuple(values)):
                refs = dict(zip(names, refs, strict=True))
                for way in range(2):
                    head, tail = (0, chain - 1) if way == 0 else (chain - 1, 0)
                    if p >= 2:
                        extra = jnp.where(early(row) == (way == 0), refs["turns", 0][p - 2], refs["turns", 1][p - 2])
                        if relay and p == 3:
                            extra = jnp.where(row == tail, refs["swapped", 1][1 - way], extra)
                        extra = jnp.where(column == 1 - way, extra, 0.0)
                    elif relay and p == 0:
                        extra = jnp.where(early(row) == (way == 0), refs["got", (0, 4)][...], refs["swapped", 0][...])
                        extra = jnp.where(row == head, refs["turns", 1][0], extra)
                    else:
                        extra = refs["swapped", p][way]
                    if p < 2:
                        extra = jnp.where((row == head) & (column == way), 0.0, extra)
                    yield extra + chained(p, way, row, [refs["got", k] for k in keys], keys)

            jobs.append((total, p * size, run[p], local[p], list(values.values())))
        outs[0], token = across(jobs, outs[0], arrays[0].shape, size, last)
        last[:] = [token]

    steps = {"F": begin, "L": bring, "S": share, "X": trade, "E": functools.partial(hop, 0), "O": functools.partial(hop, 1), "W": inside, "A": finish}
    order = [(name[0], [int(n) for n in name[1:]]) for name in ORDER]
    if chain != 4:
        order = [("L", [2, 3]), ("L", [0, 1]), ("S", [0]), ("S", [1])]
        order += [("W", [p, n]) for p in range(parts) for n in range(pieces)]
        order += [(kind, [t]) for t in range(parts + chain - 2) for kind in "EO"]
        order += [("X", [0]), ("X", [1]), ("A", [2, 3]), ("A", [0, 1])]
    for kind, numbers in order:
        steps[kind](*numbers)
    return tuple(outs[0])


def solution(mesh):
    spec = P("ctx", "seq")
    return jax.shard_map(body, mesh=mesh, in_specs=(spec,) * 4, out_specs=(spec,) * 4, check_vma=False)
```

```python
import functools

import jax
import jax.numpy as jnp
from jax import lax
from jax.experimental import pallas as pl
from jax.experimental.pallas import tpu as pltpu
from jax.sharding import PartitionSpec as P

DH = 128
F32 = jnp.float32
BF16 = jnp.bfloat16
ROWS = ((0,), (0,))
LANES = ((1,), (1,))
PLAIN = ((1,), (0,))
VMEM = pl.BlockSpec(memory_space=pltpu.VMEM)
HBM = pl.BlockSpec(memory_space=pltpu.HBM)
ACROSS_ROWS = 256
ORDER = (
    "F", "E0", "S0", "L0123", "E1", "O1", "W20", "S1", "W21", "O2", "E2", "W00", "W01", "W10",
    "E3", "O3", "X0", "W11", "O4", "X10", "E4", "X11", "W30", "W31", "E5", "A0", "A2", "B31",
    "C31",
)
PARAMS = pltpu.CompilerParams(vmem_limit_bytes=8 << 20)


def cost(us):
    return pl.CostEstimate(flops=int(us * 1.15e9), transcendentals=0, bytes_accessed=1)


def dot(a, b, dims):
    return lax.dot_general(a, b, (dims, ((), ())), preferred_element_type=F32)


def kept(arrays):
    return [pltpu.with_memory_space_constraint(a, pltpu.VMEM) for a in arrays]


def any_of(place, places):
    return functools.reduce(jnp.logical_or, [place == p for p in places])


def spot():
    place = lax.axis_index("ctx")
    return place // 2, place % 2


def first_kernel(firsts, chain, q_hbm, k_hbm, v_hbm, g_hbm, opening_ref, shared_ref, a_ref, b_ref, sems):
    row, _ = spot()
    size = opening_ref.shape[0]
    upper = row < chain // 2

    def moves(a_hbm, b_hbm):
        for n, first in enumerate(firsts):
            there = pl.ds(first * DH, size * DH)
            yield pltpu.make_async_copy(a_hbm.at[:, there], a_ref.at[n], sems.at[n, 0])
            yield pltpu.make_async_copy(b_hbm.at[:, there], b_ref.at[n], sems.at[n, 1])

    @pl.when(upper)
    def _():
        for move in moves(k_hbm, v_hbm):
            move.start()

    @pl.when(jnp.logical_not(upper))
    def _():
        for move in moves(q_hbm, g_hbm):
            move.start()

    waits = list(moves(k_hbm, v_hbm))
    for n, out in enumerate((opening_ref, shared_ref.at[0], shared_ref.at[1])):
        waits[2 * n].wait()
        waits[2 * n + 1].wait()
        for h in range(size):
            cols = slice(h * DH, (h + 1) * DH)
            out[h] = dot(a_ref[n, :, cols], b_ref[n, :, cols], ROWS)


def first_states(arrays, firsts, size, chain):
    block = (3, arrays[0].shape[0], size * DH)
    return pl.pallas_call(
        functools.partial(first_kernel, firsts, chain),
        in_specs=[HBM] * 4,
        out_specs=[VMEM] * 2,
        out_shape=[pltpu.VMEM((size, DH, DH), F32), pltpu.VMEM((2, size, DH, DH), F32)],
        scratch_shapes=[pltpu.VMEM(block, BF16), pltpu.VMEM(block, BF16), pltpu.SemaphoreType.DMA((3, 2))],
        compiler_params=PARAMS,
        cost_estimate=cost(2.5),
        name="first",
    )(*[pltpu.with_memory_space_constraint(a, pltpu.HBM) for a in arrays])


def load_kernel(firsts, q_hbm, k_hbm, v_hbm, g_hbm, *refs):
    *refs, sems = refs
    parts = [refs[len(refs) - 5 * (len(firsts) - n) :][:5] for n in range(len(firsts))]
    moves = []
    for n, (first, part) in enumerate(zip(firsts, parts, strict=True)):
        there = pl.ds(first * DH, part[0].shape[1])
        pairs = ((k_hbm, part[1]), (v_hbm, part[2]), (q_hbm, part[0]), (g_hbm, part[3]))
        moves.append([pltpu.make_async_copy(src.at[:, there], dst, sems.at[n, i]) for i, (src, dst) in enumerate(pairs)])
        for move in moves[-1]:
            move.start()
    for part, own in zip(parts, moves, strict=True):
        q_ref, k_ref, v_ref, g_ref, state_ref = part
        size = state_ref.shape[1]
        cols = [slice(h * DH, (h + 1) * DH) for h in range(size)]
        own[0].wait()
        own[1].wait()
        for h in range(size):
            state_ref[0, h] = dot(k_ref[:, cols[h]], v_ref[:, cols[h]], ROWS)
        own[2].wait()
        own[3].wait()
        for h in range(size):
            state_ref[1, h] = dot(q_ref[:, cols[h]], g_ref[:, cols[h]], ROWS)


def load(arrays, firsts, size, after):
    rows = arrays[0].shape[0]
    part = [pltpu.VMEM((rows, size * DH), BF16)] * 4 + [pltpu.VMEM((2, size, DH, DH), F32)]
    return pl.pallas_call(
        functools.partial(load_kernel, firsts),
        in_specs=[HBM] * 4 + [VMEM] * len(after),
        out_specs=[VMEM] * (5 * len(firsts)),
        out_shape=part * len(firsts),
        scratch_shapes=[pltpu.SemaphoreType.DMA((len(firsts), 4))],
        compiler_params=PARAMS,
        cost_estimate=cost(1.5 + 0.5 * len(firsts)),
        name="load",
    )(*[pltpu.with_memory_space_constraint(a, pltpu.HBM) for a in arrays], *kept(after))


def within_kernel(tile, first, *refs):
    q_ref, k_ref, v_ref, g_ref = refs[:4]
    attended_ref, query_ref, key_ref, value_ref = refs[-4:]
    rows, width = attended_ref.shape
    count = rows // tile
    causal = lax.broadcasted_iota(jnp.int32, (tile, tile), 1) <= lax.broadcasted_iota(jnp.int32, (tile, tile), 0)

    @pl.loop(0, width // DH)
    def _(h):
        lanes, source = (pl.ds(pl.multiple_of(n * DH, DH), DH) for n in (h, first + h))
        at = [pl.ds(i * tile, tile) for i in range(count)]
        q, k, v, g = ([ref[a, source] for a in at] for ref in (q_ref, k_ref, v_ref, g_ref))
        attn, grads = {}, {}
        for i in range(count):
            for j in range(i + 1):
                a, b = dot(q[i], k[j], LANES), dot(g[i], v[j], LANES)
                if i == j:
                    a, b = jnp.where(causal, a, 0.0), jnp.where(causal, b, 0.0)
                attn[i, j], grads[i, j] = a.astype(BF16), b.astype(BF16)
        for i in range(count):
            attended_ref[at[i], lanes] = sum(dot(attn[i, j], v[j], PLAIN) for j in range(i + 1))
            query_ref[at[i], lanes] = sum(dot(grads[i, j], k[j], PLAIN) for j in range(i + 1))
        for j in range(count):
            key_ref[at[j], lanes] = sum(dot(grads[i, j], q[i], ROWS) for i in range(j, count))
            value_ref[at[j], lanes] = sum(dot(attn[i, j], g[i], ROWS) for i in range(j, count))


def within(run, first, width, after):
    rows = run[0].shape[0]
    return pl.pallas_call(
        functools.partial(within_kernel, min(rows, 256), first),
        in_specs=[VMEM] * (4 + len(after)),
        out_specs=[VMEM] * 4,
        out_shape=[pltpu.VMEM((rows, width), F32)] * 4,
        compiler_params=PARAMS,
        cost_estimate=cost(1.5),
        name="within",
    )(*kept(run), *kept(after))


def mix(function, shape, arrays, after, name):
    def kernel(*refs):
        row, column = spot()
        function(row, column, refs[: len(arrays)], refs[-1])

    return pl.pallas_call(
        kernel,
        in_specs=[VMEM] * (len(arrays) + len(after)),
        out_specs=VMEM,
        out_shape=pltpu.VMEM(shape, F32),
        compiler_params=PARAMS,
        cost_estimate=cost(3),
        name=name,
    )(*kept(arrays), *kept(after))


def across_kernel(turn, chain, jobs, *refs):
    *outs, token_ref, done_ref, sems = refs[-7:]
    row, column = spot()
    ready = []
    for total, first, pieces, count in jobs:
        run, refs = refs[:4], refs[4:]
        parts, refs = [refs[4 * n : 4 * n + 4] for n in range(pieces)], refs[4 * pieces :]
        sources, refs = refs[:count], refs[count:]
        ready.append((run, parts, first, [value.astype(BF16) for value in total(row, column, sources)]))
    _, slots, rows, width = done_ref.shape
    block = min(rows, ACROSS_ROWS)

    def copy(n, i, start, out):
        here = pl.ds(start, block)
        there = out.at[here, pl.ds(ready[n][2] * DH, width)]
        return pltpu.make_async_copy(done_ref.at[n, i, here], there, sems.at[n, i, start // block])

    def write(base):
        for n, ((q_ref, k_ref, v_ref, g_ref), parts, _, states) in enumerate(ready):
            wide = width // len(parts)
            factors = ((q_ref, PLAIN), (g_ref, LANES), (v_ref, LANES), (k_ref, PLAIN))
            for start in range(0, rows, block):
                here = pl.ds(start, block)
                for i in range(slots):
                    factor, dims = factors[base + i]
                    state = states[i // 2]
                    for at in range(0, width, DH):
                        part = parts[at // wide][base + i][here, pl.ds(at % wide, DH)]
                        term = dot(factor[here, pl.ds(at, DH)], state[at // DH], dims)
                        done_ref[n, i, here, pl.ds(at, DH)] = (part + term).astype(BF16)
                    copy(n, i, start, outs[base + i]).start()

    if turn is None:
        write(0)
    else:
        upper = (row < chain // 2) == (turn == 0)
        pl.when(upper)(lambda: write(0))
        pl.when(jnp.logical_not(upper))(lambda: write(2))
    token_ref[...] = jnp.zeros_like(token_ref)
    for n in range(len(ready)):
        for start in range(0, rows, block):
            for i in range(slots):
                copy(n, i, start, outs[i]).wait()


def across(jobs, turn, chain, outs, shape, size, after):
    held = () if outs is None else tuple(outs)
    arrays = [a for _, _, run, parts, sources in jobs for a in [*run, *sum(map(list, parts), []), *sources]]
    slots = 4 if turn is None else 2
    *outs, token = pl.pallas_call(
        functools.partial(
            across_kernel,
            turn,
            chain,
            [(total, first, len(parts), len(sources)) for total, first, _, parts, sources in jobs],
        ),
        in_specs=[VMEM] * len(arrays) + [HBM] * len(held) + [VMEM] * len(after),
        out_specs=[HBM] * 4 + [VMEM],
        out_shape=[jax.ShapeDtypeStruct(shape, BF16)] * 4 + [pltpu.VMEM((8, DH), F32)],
        input_output_aliases={len(arrays) + i: i for i in range(len(held))},
        scratch_shapes=[
            pltpu.VMEM((len(jobs), slots, shape[0], size * DH), BF16),
            pltpu.SemaphoreType.DMA((len(jobs), slots, max(1, shape[0] // ACROSS_ROWS))),
        ],
        compiler_params=PARAMS,
        cost_estimate=cost(0.4 * slots * len(jobs)),
        name="across",
    )(*kept(arrays), *held, *kept(after))
    return outs, token


def body(*arrays):
    heads = arrays[0].shape[1] // DH
    runs, groups_of_heads = lax.axis_size("ctx"), lax.axis_size("seq")
    chain = runs // 2
    relay = chain == 4
    parts = 4
    size = heads // parts
    shape = (size, DH, DH)
    run = [[None] * 4 for _ in range(parts)]
    own = [None] * parts
    pieces = min(size, 2)
    local = [[None] * pieces for _ in range(parts)]
    got, turns, swapped = {}, {}, {}
    last, opening = [], []
    pair = [(r, r ^ 1) for r in range(runs)]

    def early(row):
        return row < chain // 2

    def near(row, column):
        return ((row == 0) & (column == 0)) | ((row == chain - 1) & (column == 1))

    def end(row):
        return (row == 0) | (row == chain - 1)

    def far(row, column):
        return end(row) & jnp.logical_not(near(row, column))

    def swap(parity):
        perm = []
        for r in range(runs):
            z, c = r // 2, r % 2
            mate = z + 1 if z % 2 == parity else z - 1
            for s in range(groups_of_heads):
                if 0 <= mate < chain:
                    to = (2 * mate + c) * groups_of_heads + s
                else:
                    to = r * groups_of_heads + (s ^ 1)
                perm.append((r * groups_of_heads + s, to))
        return perm

    def arrival(p, z, way):
        if way == 0:
            return None if z == 0 else ((z - 1) % 2, p + z - 1)
        return None if z == chain - 1 else (z % 2, p + chain - 2 - z)

    def bring(*chosen):
        found = load(arrays, [p * size for p in chosen], size, last)
        for n, p in enumerate(chosen):
            *run[p], own[p] = found[5 * n : 5 * n + 5]
        last[:] = [own[chosen[0]]]

    def begin():
        opening[:] = first_states(arrays, [p * size for p in (0, 2, 3)], size, chain)
        last[:] = [opening[0]]

    def inside(p, piece):
        wide = max(1, size // 2)
        local[p][piece] = within(run[p], piece * wide, wide * DH, last)
        last[:] = [local[p][piece][0]]

    def share(turn):
        if opening and not turn:
            turns[0] = lax.ppermute(opening[1], "ctx", pair)
            return
        values = [own[2], own[3]]
        if turn and relay:
            values += [own[0], got[0, 0]]

        def function(row, column, refs, out):
            for n in range(2):
                first, then = refs[n][0], refs[n][1]
                value = jnp.where(early(row), *((then, first) if turn else (first, then)))
                if turn and relay:
                    mine = jnp.where(early(row), refs[2][0], refs[2][1])
                    value = jnp.where(near(row, column), mine + refs[3][...] if n else mine, value)
                    if n:
                        value = jnp.where(far(row, column), mine, value)
                out[n] = value

        payload = mix(function, (2,) + shape, values, last, "share")
        last[:] = [payload]
        turns[turn] = lax.ppermute(payload, "ctx", pair)

    def keys_of(p, turn):
        places = [(z, way) for z in range(chain) for way in range(2) if turn in (None, turn_of(way, z))]
        return sorted({arrival(p, z, way) for z, way in places} - {None})

    def turn_of(way, z):
        return 0 if early(z) == (way == 0) else 1

    def trade(p, turn=None):
        turn = 1 if relay and p == 0 else turn
        keys = keys_of(p, turn)
        late = relay and p == 1 and turn == 0
        values = [own[p]] + [got[k] for k in keys] + ([own[3]] if late else [])

        def function(row, column, refs, out):
            sums = []
            for way in range(2):
                value = jnp.where(column == way, refs[0][way], 0.0) + chained(p, way, row, refs[1:], keys)
                if late:
                    spare = (row == (0, chain - 1)[way]) & (column == 1 - way)
                    value = jnp.where(spare, refs[-1][1 - way], value)
                sums.append(value)
            if turn is None:
                out[0], out[1] = sums
            else:
                out[...] = jnp.where(early(row) == (turn == 0), *sums)

        payload = mix(function, (2,) + shape if turn is None else shape, values, last, "trade")
        last[:] = [payload]
        swapped[p, turn] = lax.ppermute(payload, "ctx", pair)

    def chained(p, way, row, refs, keys):
        total = jnp.zeros(shape, F32)
        for key, ref in zip(keys, refs):
            places = [z for z in range(chain) if arrival(p, z, way) == key]
            if places:
                total = jnp.where(any_of(row, places), ref[...], total)
        return total

    def hop(parity, slot):
        groups = {}
        for link in range(parity, chain - 1, 2):
            for way, p, z in ((0, slot - link, link), (1, slot - (chain - 2 - link), link + 1)):
                if 0 <= p < parts:
                    groups.setdefault((p, arrival(p, z, way)), ([], []))[way].append(z)
        if not groups:
            return
        forward = relay and parity == 0 and slot == 4
        names = []
        for (p, key), ways in groups.items():
            names.append(("own", p))
            if p >= 2:
                names += [("turns", turn_of(way, z)) for way in range(2) for z in ways[way]]
            if key is not None:
                names.append(("got", key))
        if forward:
            names.append(("turns", 1))
        names = list(dict.fromkeys(names))
        tables = {"own": own, "turns": turns, "got": got}
        values = [tables[kind][key] for kind, key in names]

        def function(row, column, refs, out):
            refs = dict(zip(names, refs, strict=True))

            def state(p, way, rows):
                value = refs["own", p][way]
                if p >= 2:
                    found = {turn_of(way, z) for z in rows}
                    ways = [refs["turns", turn][p - 2] if turn in found else None for turn in range(2)]
                    if len(found) == 2:
                        other = jnp.where(early(row) == (way == 0), *ways)
                    else:
                        other = ways[found.pop()]
                    value = value + other
                return value

            payload = None
            for (p, key), (up, down) in groups.items():
                if up and down:
                    rising = early(row) if relay and slot == 0 else any_of(row, up)
                    value = jnp.where(rising, state(p, 0, up), state(p, 1, down))
                else:
                    value = state(p, 0, up) if up else state(p, 1, down)
                if key is not None:
                    value = value + refs["got", key][...]
                payload = value if payload is None else jnp.where(any_of(row, up + down), value, payload)
            if forward:
                payload = jnp.where(end(row), refs["turns", 1][1], payload)
            out[...] = payload

        if opening and (parity, slot) == (0, 0):
            payload = opening[0]
        else:
            payload = mix(function, shape, values, last, "hop")
            last[:] = [payload]
        got[parity, slot] = lax.ppermute(payload, ("ctx", "seq"), swap(parity))

    outs = [None]

    def finish(turn, *chosen):
        jobs = []
        for p in chosen:
            keys = keys_of(p, turn)
            values = {("got", k): got[k] for k in keys}
            if p >= 2:
                values |= {("turns", n): turns[n] for n in range(2) if turn in (None, n)}
            elif relay and p == 1:
                values |= {("swapped", (1, n)): swapped[1, n] for n in range(2) if turn in (None, n)}
            elif relay:
                values |= {("swapped", (0, 1)): swapped[0, 1], ("turns", 1): turns[1], ("got", (0, 4)): got[0, 4]}
            else:
                values["swapped", (p, None)] = swapped[p, None]
            if relay and p == 3 and turn != 0:
                values["swapped", (1, 0)] = swapped[1, 0]

            def total(row, column, refs, p=p, keys=keys, names=tuple(values)):
                refs = dict(zip(names, refs, strict=True))
                sums = []
                for way in range(2):
                    head, tail = (0, chain - 1) if way == 0 else (chain - 1, 0)

                    def chosen_of(kind, pick):
                        if turn is not None:
                            return pick(refs[kind(turn)])
                        return jnp.where(early(row) == (way == 0), pick(refs[kind(0)]), pick(refs[kind(1)]))

                    if p >= 2:
                        extra = chosen_of(lambda n: ("turns", n), lambda ref: ref[p - 2])
                        if relay and p == 3 and turn != 0:
                            extra = jnp.where(row == tail, refs["swapped", (1, 0)][...], extra)
                        extra = jnp.where(column == 1 - way, extra, 0.0)
                    elif relay and p == 1:
                        extra = chosen_of(lambda n: ("swapped", (1, n)), lambda ref: ref[...])
                    elif relay:
                        extra = jnp.where(early(row) == (way == 0), refs["got", (0, 4)][...], refs["swapped", (0, 1)][...])
                        extra = jnp.where(row == head, refs["turns", 1][0], extra)
                    else:
                        extra = refs["swapped", (p, None)][way]
                    if p < 2:
                        extra = jnp.where((row == head) & (column == way), 0.0, extra)
                    sums.append(extra + chained(p, way, row, [refs["got", k] for k in keys], keys))
                return sums if turn is None else [jnp.where(early(row) == (turn == 0), *sums)]

            jobs.append((total, p * size, run[p], local[p], list(values.values())))
        outs[0], token = across(jobs, turn, chain, outs[0], arrays[0].shape, size, last)
        last[:] = [token]

    steps = {"F": begin, "L": bring, "S": share, "X": trade, "E": functools.partial(hop, 0), "O": functools.partial(hop, 1), "W": inside, "A": functools.partial(finish, None)}
    steps |= {"B": functools.partial(finish, 0), "C": functools.partial(finish, 1)}
    order = [(name[0], [int(n) for n in name[1:]]) for name in ORDER]
    if chain != 4:
        order = [("L", [2, 3]), ("L", [0, 1]), ("S", [0]), ("S", [1])]
        order += [("W", [p, n]) for p in range(parts) for n in range(pieces)]
        order += [(kind, [t]) for t in range(parts + chain - 2) for kind in "EO"]
        order += [("X", [0]), ("X", [1]), ("A", [2, 3]), ("A", [0, 1])]
    for kind, numbers in order:
        steps[kind](*numbers)
    return tuple(outs[0])


def solution(mesh):
    spec = P("ctx", "seq")
    return jax.shard_map(body, mesh=mesh, in_specs=(spec,) * 4, out_specs=(spec,) * 4, check_vma=False)
```

```python
import functools

import jax
import jax.numpy as jnp
from jax import lax
from jax.experimental import pallas as pl
from jax.experimental.pallas import tpu as pltpu
from jax.sharding import PartitionSpec as P

DH = 128
F32 = jnp.float32
BF16 = jnp.bfloat16
ROWS = ((0,), (0,))
LANES = ((1,), (1,))
PLAIN = ((1,), (0,))
VMEM = pl.BlockSpec(memory_space=pltpu.VMEM)
HBM = pl.BlockSpec(memory_space=pltpu.HBM)
ACROSS_ROWS = 256
ORDER = (
    "F", "E0", "S0", "L0123", "E1", "O1", "W20", "S1", "W21", "O2", "E2", "W00", "W01", "W10",
    "E3", "O3", "X0", "W11", "O4", "X10", "E4", "X11", "W30", "W31", "E5", "A02", "B31",
    "C31",
)
PARAMS = pltpu.CompilerParams(vmem_limit_bytes=8 << 20)


def cost(us):
    return pl.CostEstimate(flops=int(us * 1.15e9), transcendentals=0, bytes_accessed=1)


def dot(a, b, dims):
    return lax.dot_general(a, b, (dims, ((), ())), preferred_element_type=F32)


def kept(arrays):
    return [pltpu.with_memory_space_constraint(a, pltpu.VMEM) for a in arrays]


def any_of(place, places):
    return functools.reduce(jnp.logical_or, [place == p for p in places])


def spot():
    place = lax.axis_index("ctx")
    return place // 2, place % 2


def first_kernel(firsts, chain, q_hbm, k_hbm, v_hbm, g_hbm, opening_ref, shared_ref, a_ref, b_ref, sems):
    row, _ = spot()
    size = opening_ref.shape[0]
    upper = row < chain // 2

    def moves(a_hbm, b_hbm):
        for n, first in enumerate(firsts):
            there = pl.ds(first * DH, size * DH)
            yield pltpu.make_async_copy(a_hbm.at[:, there], a_ref.at[n], sems.at[n, 0])
            yield pltpu.make_async_copy(b_hbm.at[:, there], b_ref.at[n], sems.at[n, 1])

    @pl.when(upper)
    def _():
        for move in moves(k_hbm, v_hbm):
            move.start()

    @pl.when(jnp.logical_not(upper))
    def _():
        for move in moves(q_hbm, g_hbm):
            move.start()

    waits = list(moves(k_hbm, v_hbm))
    for n, out in enumerate((opening_ref, shared_ref.at[0], shared_ref.at[1])):
        waits[2 * n].wait()
        waits[2 * n + 1].wait()
        for h in range(size):
            cols = slice(h * DH, (h + 1) * DH)
            out[h] = dot(a_ref[n, :, cols], b_ref[n, :, cols], ROWS)


def first_states(arrays, firsts, size, chain):
    block = (3, arrays[0].shape[0], size * DH)
    return pl.pallas_call(
        functools.partial(first_kernel, firsts, chain),
        in_specs=[HBM] * 4,
        out_specs=[VMEM] * 2,
        out_shape=[pltpu.VMEM((size, DH, DH), F32), pltpu.VMEM((2, size, DH, DH), F32)],
        scratch_shapes=[pltpu.VMEM(block, BF16), pltpu.VMEM(block, BF16), pltpu.SemaphoreType.DMA((3, 2))],
        compiler_params=PARAMS,
        cost_estimate=cost(2.5),
        name="first",
    )(*[pltpu.with_memory_space_constraint(a, pltpu.HBM) for a in arrays])


def load_kernel(firsts, q_hbm, k_hbm, v_hbm, g_hbm, *refs):
    *refs, sems = refs
    parts = [refs[len(refs) - 5 * (len(firsts) - n) :][:5] for n in range(len(firsts))]
    moves = []
    for n, (first, part) in enumerate(zip(firsts, parts, strict=True)):
        there = pl.ds(first * DH, part[0].shape[1])
        pairs = ((k_hbm, part[1]), (v_hbm, part[2]), (q_hbm, part[0]), (g_hbm, part[3]))
        moves.append([pltpu.make_async_copy(src.at[:, there], dst, sems.at[n, i]) for i, (src, dst) in enumerate(pairs)])
        for move in moves[-1]:
            move.start()
    for part, own in zip(parts, moves, strict=True):
        q_ref, k_ref, v_ref, g_ref, state_ref = part
        size = state_ref.shape[1]
        cols = [slice(h * DH, (h + 1) * DH) for h in range(size)]
        own[0].wait()
        own[1].wait()
        for h in range(size):
            state_ref[0, h] = dot(k_ref[:, cols[h]], v_ref[:, cols[h]], ROWS)
        own[2].wait()
        own[3].wait()
        for h in range(size):
            state_ref[1, h] = dot(q_ref[:, cols[h]], g_ref[:, cols[h]], ROWS)


def load(arrays, firsts, size, after):
    rows = arrays[0].shape[0]
    part = [pltpu.VMEM((rows, size * DH), BF16)] * 4 + [pltpu.VMEM((2, size, DH, DH), F32)]
    return pl.pallas_call(
        functools.partial(load_kernel, firsts),
        in_specs=[HBM] * 4 + [VMEM] * len(after),
        out_specs=[VMEM] * (5 * len(firsts)),
        out_shape=part * len(firsts),
        scratch_shapes=[pltpu.SemaphoreType.DMA((len(firsts), 4))],
        compiler_params=PARAMS,
        cost_estimate=cost(1.5 + 0.5 * len(firsts)),
        name="load",
    )(*[pltpu.with_memory_space_constraint(a, pltpu.HBM) for a in arrays], *kept(after))


def within_kernel(tile, first, *refs):
    q_ref, k_ref, v_ref, g_ref = refs[:4]
    attended_ref, query_ref, key_ref, value_ref = refs[-4:]
    rows, width = attended_ref.shape
    count = rows // tile
    causal = lax.broadcasted_iota(jnp.int32, (tile, tile), 1) <= lax.broadcasted_iota(jnp.int32, (tile, tile), 0)

    @pl.loop(0, width // DH)
    def _(h):
        lanes, source = (pl.ds(pl.multiple_of(n * DH, DH), DH) for n in (h, first + h))
        at = [pl.ds(i * tile, tile) for i in range(count)]
        q, k, v, g = ([ref[a, source] for a in at] for ref in (q_ref, k_ref, v_ref, g_ref))
        attn, grads = {}, {}
        for i in range(count):
            for j in range(i + 1):
                a, b = dot(q[i], k[j], LANES), dot(g[i], v[j], LANES)
                if i == j:
                    a, b = jnp.where(causal, a, 0.0), jnp.where(causal, b, 0.0)
                attn[i, j], grads[i, j] = a.astype(BF16), b.astype(BF16)
        for i in range(count):
            attended_ref[at[i], lanes] = sum(dot(attn[i, j], v[j], PLAIN) for j in range(i + 1))
            query_ref[at[i], lanes] = sum(dot(grads[i, j], k[j], PLAIN) for j in range(i + 1))
        for j in range(count):
            key_ref[at[j], lanes] = sum(dot(grads[i, j], q[i], ROWS) for i in range(j, count))
            value_ref[at[j], lanes] = sum(dot(attn[i, j], g[i], ROWS) for i in range(j, count))


def within(run, first, width, after):
    rows = run[0].shape[0]
    return pl.pallas_call(
        functools.partial(within_kernel, min(rows, 256), first),
        in_specs=[VMEM] * (4 + len(after)),
        out_specs=[VMEM] * 4,
        out_shape=[pltpu.VMEM((rows, width), F32)] * 4,
        compiler_params=PARAMS,
        cost_estimate=cost(1.5),
        name="within",
    )(*kept(run), *kept(after))


def mix(function, shape, arrays, after, name):
    def kernel(*refs):
        row, column = spot()
        function(row, column, refs[: len(arrays)], refs[-1])

    return pl.pallas_call(
        kernel,
        in_specs=[VMEM] * (len(arrays) + len(after)),
        out_specs=VMEM,
        out_shape=pltpu.VMEM(shape, F32),
        compiler_params=PARAMS,
        cost_estimate=cost(3),
        name=name,
    )(*kept(arrays), *kept(after))


def across_kernel(turn, chain, jobs, *refs):
    *outs, token_ref, done_ref, sems = refs[-7:]
    row, column = spot()
    ready = []
    for total, first, pieces, count in jobs:
        run, refs = refs[:4], refs[4:]
        parts, refs = [refs[4 * n : 4 * n + 4] for n in range(pieces)], refs[4 * pieces :]
        sources, refs = refs[:count], refs[count:]
        ready.append((run, parts, first, [value.astype(BF16) for value in total(row, column, sources)]))
    _, slots, rows, width = done_ref.shape
    block = min(rows, ACROSS_ROWS)

    def copy(n, i, start, out):
        here = pl.ds(start, block)
        there = out.at[here, pl.ds(ready[n][2] * DH, width)]
        return pltpu.make_async_copy(done_ref.at[n, i, here], there, sems.at[n, i, start // block])

    def write(base):
        for n, ((q_ref, k_ref, v_ref, g_ref), parts, _, states) in enumerate(ready):
            wide = width // len(parts)
            factors = ((q_ref, PLAIN), (g_ref, LANES), (v_ref, LANES), (k_ref, PLAIN))
            for start in range(0, rows, block):
                here = pl.ds(start, block)
                for i in range(slots):
                    factor, dims = factors[base + i]
                    state = states[i // 2]
                    for at in range(0, width, DH):
                        part = parts[at // wide][base + i][here, pl.ds(at % wide, DH)]
                        term = dot(factor[here, pl.ds(at, DH)], state[at // DH], dims)
                        done_ref[n, i, here, pl.ds(at, DH)] = (part + term).astype(BF16)
                    copy(n, i, start, outs[base + i]).start()

    if turn is None:
        write(0)
    else:
        upper = (row < chain // 2) == (turn == 0)
        pl.when(upper)(lambda: write(0))
        pl.when(jnp.logical_not(upper))(lambda: write(2))
    token_ref[...] = jnp.zeros_like(token_ref)
    for n in range(len(ready)):
        for start in range(0, rows, block):
            for i in range(slots):
                copy(n, i, start, outs[i]).wait()


def across(jobs, turn, chain, outs, shape, size, after):
    held = () if outs is None else tuple(outs)
    arrays = [a for _, _, run, parts, sources in jobs for a in [*run, *sum(map(list, parts), []), *sources]]
    slots = 4 if turn is None else 2
    *outs, token = pl.pallas_call(
        functools.partial(
            across_kernel,
            turn,
            chain,
            [(total, first, len(parts), len(sources)) for total, first, _, parts, sources in jobs],
        ),
        in_specs=[VMEM] * len(arrays) + [HBM] * len(held) + [VMEM] * len(after),
        out_specs=[HBM] * 4 + [VMEM],
        out_shape=[jax.ShapeDtypeStruct(shape, BF16)] * 4 + [pltpu.VMEM((8, DH), F32)],
        input_output_aliases={len(arrays) + i: i for i in range(len(held))},
        scratch_shapes=[
            pltpu.VMEM((len(jobs), slots, shape[0], size * DH), BF16),
            pltpu.SemaphoreType.DMA((len(jobs), slots, max(1, shape[0] // ACROSS_ROWS))),
        ],
        compiler_params=PARAMS,
        cost_estimate=cost(0.4 * slots * len(jobs)),
        name="across",
    )(*kept(arrays), *held, *kept(after))
    return outs, token


def body(*arrays):
    heads = arrays[0].shape[1] // DH
    runs, groups_of_heads = lax.axis_size("ctx"), lax.axis_size("seq")
    chain = runs // 2
    relay = chain == 4
    parts = 4
    size = heads // parts
    shape = (size, DH, DH)
    run = [[None] * 4 for _ in range(parts)]
    own = [None] * parts
    pieces = min(size, 2)
    local = [[None] * pieces for _ in range(parts)]
    got, turns, swapped = {}, {}, {}
    last, opening = [], []
    pair = [(r, r ^ 1) for r in range(runs)]

    def early(row):
        return row < chain // 2

    def near(row, column):
        return ((row == 0) & (column == 0)) | ((row == chain - 1) & (column == 1))

    def end(row):
        return (row == 0) | (row == chain - 1)

    def far(row, column):
        return end(row) & jnp.logical_not(near(row, column))

    def swap(parity):
        perm = []
        for r in range(runs):
            z, c = r // 2, r % 2
            mate = z + 1 if z % 2 == parity else z - 1
            for s in range(groups_of_heads):
                if 0 <= mate < chain:
                    to = (2 * mate + c) * groups_of_heads + s
                else:
                    to = r * groups_of_heads + (s ^ 1)
                perm.append((r * groups_of_heads + s, to))
        return perm

    def arrival(p, z, way):
        if way == 0:
            return None if z == 0 else ((z - 1) % 2, p + z - 1)
        return None if z == chain - 1 else (z % 2, p + chain - 2 - z)

    def bring(*chosen):
        found = load(arrays, [p * size for p in chosen], size, last)
        for n, p in enumerate(chosen):
            *run[p], own[p] = found[5 * n : 5 * n + 5]
        last[:] = [own[chosen[0]]]

    def begin():
        opening[:] = first_states(arrays, [p * size for p in (0, 2, 3)], size, chain)
        last[:] = [opening[0]]

    def inside(p, piece):
        wide = max(1, size // 2)
        local[p][piece] = within(run[p], piece * wide, wide * DH, last)
        last[:] = [local[p][piece][0]]

    def share(turn):
        if opening and not turn:
            turns[0] = lax.ppermute(opening[1], "ctx", pair)
            return
        values = [own[2], own[3]]
        if turn and relay:
            values += [own[0], got[0, 0]]

        def function(row, column, refs, out):
            for n in range(2):
                first, then = refs[n][0], refs[n][1]
                value = jnp.where(early(row), *((then, first) if turn else (first, then)))
                if turn and relay:
                    mine = jnp.where(early(row), refs[2][0], refs[2][1])
                    value = jnp.where(near(row, column), mine + refs[3][...] if n else mine, value)
                    if n:
                        value = jnp.where(far(row, column), mine, value)
                out[n] = value

        payload = mix(function, (2,) + shape, values, last, "share")
        last[:] = [payload]
        turns[turn] = lax.ppermute(payload, "ctx", pair)

    def keys_of(p, turn):
        places = [(z, way) for z in range(chain) for way in range(2) if turn in (None, turn_of(way, z))]
        return sorted({arrival(p, z, way) for z, way in places} - {None})

    def turn_of(way, z):
        return 0 if early(z) == (way == 0) else 1

    def trade(p, turn=None):
        turn = 1 if relay and p == 0 else turn
        keys = keys_of(p, turn)
        late = relay and p == 1 and turn == 0
        values = [own[p]] + [got[k] for k in keys] + ([own[3]] if late else [])

        def function(row, column, refs, out):
            sums = []
            for way in range(2):
                value = jnp.where(column == way, refs[0][way], 0.0) + chained(p, way, row, refs[1:], keys)
                if late:
                    spare = (row == (0, chain - 1)[way]) & (column == 1 - way)
                    value = jnp.where(spare, refs[-1][1 - way], value)
                sums.append(value)
            if turn is None:
                out[0], out[1] = sums
            else:
                out[...] = jnp.where(early(row) == (turn == 0), *sums)

        payload = mix(function, (2,) + shape if turn is None else shape, values, last, "trade")
        last[:] = [payload]
        swapped[p, turn] = lax.ppermute(payload, "ctx", pair)

    def chained(p, way, row, refs, keys):
        total = jnp.zeros(shape, F32)
        for key, ref in zip(keys, refs):
            places = [z for z in range(chain) if arrival(p, z, way) == key]
            if places:
                total = jnp.where(any_of(row, places), ref[...], total)
        return total

    def hop(parity, slot):
        groups = {}
        for link in range(parity, chain - 1, 2):
            for way, p, z in ((0, slot - link, link), (1, slot - (chain - 2 - link), link + 1)):
                if 0 <= p < parts:
                    groups.setdefault((p, arrival(p, z, way)), ([], []))[way].append(z)
        if not groups:
            return
        forward = relay and parity == 0 and slot == 4
        names = []
        for (p, key), ways in groups.items():
            names.append(("own", p))
            if p >= 2:
                names += [("turns", turn_of(way, z)) for way in range(2) for z in ways[way]]
            if key is not None:
                names.append(("got", key))
        if forward:
            names.append(("turns", 1))
        names = list(dict.fromkeys(names))
        tables = {"own": own, "turns": turns, "got": got}
        values = [tables[kind][key] for kind, key in names]

        def function(row, column, refs, out):
            refs = dict(zip(names, refs, strict=True))

            def state(p, way, rows):
                value = refs["own", p][way]
                if p >= 2:
                    found = {turn_of(way, z) for z in rows}
                    ways = [refs["turns", turn][p - 2] if turn in found else None for turn in range(2)]
                    if len(found) == 2:
                        other = jnp.where(early(row) == (way == 0), *ways)
                    else:
                        other = ways[found.pop()]
                    value = value + other
                return value

            payload = None
            for (p, key), (up, down) in groups.items():
                if up and down:
                    rising = early(row) if relay and slot == 0 else any_of(row, up)
                    value = jnp.where(rising, state(p, 0, up), state(p, 1, down))
                else:
                    value = state(p, 0, up) if up else state(p, 1, down)
                if key is not None:
                    value = value + refs["got", key][...]
                payload = value if payload is None else jnp.where(any_of(row, up + down), value, payload)
            if forward:
                payload = jnp.where(end(row), refs["turns", 1][1], payload)
            out[...] = payload

        if opening and (parity, slot) == (0, 0):
            payload = opening[0]
        else:
            payload = mix(function, shape, values, last, "hop")
            last[:] = [payload]
        got[parity, slot] = lax.ppermute(payload, ("ctx", "seq"), swap(parity))

    outs = [None]

    def finish(turn, *chosen):
        jobs = []
        for p in chosen:
            keys = keys_of(p, turn)
            values = {("got", k): got[k] for k in keys}
            if p >= 2:
                values |= {("turns", n): turns[n] for n in range(2) if turn in (None, n)}
            elif relay and p == 1:
                values |= {("swapped", (1, n)): swapped[1, n] for n in range(2) if turn in (None, n)}
            elif relay:
                values |= {("swapped", (0, 1)): swapped[0, 1], ("turns", 1): turns[1], ("got", (0, 4)): got[0, 4]}
            else:
                values["swapped", (p, None)] = swapped[p, None]
            if relay and p == 3 and turn != 0:
                values["swapped", (1, 0)] = swapped[1, 0]

            def total(row, column, refs, p=p, keys=keys, names=tuple(values)):
                refs = dict(zip(names, refs, strict=True))
                sums = []
                for way in range(2):
                    head, tail = (0, chain - 1) if way == 0 else (chain - 1, 0)

                    def chosen_of(kind, pick):
                        if turn is not None:
                            return pick(refs[kind(turn)])
                        return jnp.where(early(row) == (way == 0), pick(refs[kind(0)]), pick(refs[kind(1)]))

                    if p >= 2:
                        extra = chosen_of(lambda n: ("turns", n), lambda ref: ref[p - 2])
                        if relay and p == 3 and turn != 0:
                            extra = jnp.where(row == tail, refs["swapped", (1, 0)][...], extra)
                        extra = jnp.where(column == 1 - way, extra, 0.0)
                    elif relay and p == 1:
                        extra = chosen_of(lambda n: ("swapped", (1, n)), lambda ref: ref[...])
                    elif relay:
                        extra = jnp.where(early(row) == (way == 0), refs["got", (0, 4)][...], refs["swapped", (0, 1)][...])
                        extra = jnp.where(row == head, refs["turns", 1][0], extra)
                    else:
                        extra = refs["swapped", (p, None)][way]
                    if p < 2:
                        extra = jnp.where((row == head) & (column == way), 0.0, extra)
                    sums.append(extra + chained(p, way, row, [refs["got", k] for k in keys], keys))
                return sums if turn is None else [jnp.where(early(row) == (turn == 0), *sums)]

            jobs.append((total, p * size, run[p], local[p], list(values.values())))
        outs[0], token = across(jobs, turn, chain, outs[0], arrays[0].shape, size, last)
        last[:] = [token]

    steps = {"F": begin, "L": bring, "S": share, "X": trade, "E": functools.partial(hop, 0), "O": functools.partial(hop, 1), "W": inside, "A": functools.partial(finish, None)}
    steps |= {"B": functools.partial(finish, 0), "C": functools.partial(finish, 1)}
    order = [(name[0], [int(n) for n in name[1:]]) for name in ORDER]
    if chain != 4:
        order = [("L", [2, 3]), ("L", [0, 1]), ("S", [0]), ("S", [1])]
        order += [("W", [p, n]) for p in range(parts) for n in range(pieces)]
        order += [(kind, [t]) for t in range(parts + chain - 2) for kind in "EO"]
        order += [("X", [0]), ("X", [1]), ("A", [2, 3]), ("A", [0, 1])]
    for kind, numbers in order:
        steps[kind](*numbers)
    return tuple(outs[0])


def solution(mesh):
    spec = P("ctx", "seq")
    return jax.shard_map(body, mesh=mesh, in_specs=(spec,) * 4, out_specs=(spec,) * 4, check_vma=False)
```

```python
import functools

import jax
import jax.numpy as jnp
from jax import lax
from jax.experimental import pallas as pl
from jax.experimental.pallas import tpu as pltpu
from jax.sharding import PartitionSpec as P

DH = 128
F32 = jnp.float32
BF16 = jnp.bfloat16
ROWS = ((0,), (0,))
LANES = ((1,), (1,))
PLAIN = ((1,), (0,))
VMEM = pl.BlockSpec(memory_space=pltpu.VMEM)
HBM = pl.BlockSpec(memory_space=pltpu.HBM)
ACROSS_ROWS = 256
ORDER = (
    "F", "E0", "S0", "L0123", "E1", "O1", "W20", "S1", "W21", "O2", "E2", "W00", "W01", "W10",
    "E3", "O3", "X0", "W11", "O4", "E4", "X10", "X11", "W30", "W31", "E5", "A02", "B31",
    "C31",
)
PARAMS = pltpu.CompilerParams(vmem_limit_bytes=8 << 20)


def cost(us):
    return pl.CostEstimate(flops=int(us * 1.15e9), transcendentals=0, bytes_accessed=1)


def dot(a, b, dims):
    return lax.dot_general(a, b, (dims, ((), ())), preferred_element_type=F32)


def kept(arrays):
    return [pltpu.with_memory_space_constraint(a, pltpu.VMEM) for a in arrays]


def any_of(place, places):
    return functools.reduce(jnp.logical_or, [place == p for p in places])


def spot():
    place = lax.axis_index("ctx")
    return place // 2, place % 2


def first_kernel(firsts, chain, q_hbm, k_hbm, v_hbm, g_hbm, opening_ref, shared_ref, a_ref, b_ref, sems):
    row, _ = spot()
    size = opening_ref.shape[0]
    upper = row < chain // 2

    def moves(a_hbm, b_hbm):
        for n, first in enumerate(firsts):
            there = pl.ds(first * DH, size * DH)
            yield pltpu.make_async_copy(a_hbm.at[:, there], a_ref.at[n], sems.at[n, 0])
            yield pltpu.make_async_copy(b_hbm.at[:, there], b_ref.at[n], sems.at[n, 1])

    @pl.when(upper)
    def _():
        for move in moves(k_hbm, v_hbm):
            move.start()

    @pl.when(jnp.logical_not(upper))
    def _():
        for move in moves(q_hbm, g_hbm):
            move.start()

    waits = list(moves(k_hbm, v_hbm))
    for n, out in enumerate((opening_ref, shared_ref.at[0], shared_ref.at[1])):
        waits[2 * n].wait()
        waits[2 * n + 1].wait()
        for h in range(size):
            cols = slice(h * DH, (h + 1) * DH)
            out[h] = dot(a_ref[n, :, cols], b_ref[n, :, cols], ROWS)


def first_states(arrays, firsts, size, chain):
    block = (3, arrays[0].shape[0], size * DH)
    return pl.pallas_call(
        functools.partial(first_kernel, firsts, chain),
        in_specs=[HBM] * 4,
        out_specs=[VMEM] * 2,
        out_shape=[pltpu.VMEM((size, DH, DH), F32), pltpu.VMEM((2, size, DH, DH), F32)],
        scratch_shapes=[pltpu.VMEM(block, BF16), pltpu.VMEM(block, BF16), pltpu.SemaphoreType.DMA((3, 2))],
        compiler_params=PARAMS,
        cost_estimate=cost(2.5),
        name="first",
    )(*[pltpu.with_memory_space_constraint(a, pltpu.HBM) for a in arrays])


def load_kernel(firsts, q_hbm, k_hbm, v_hbm, g_hbm, *refs):
    *refs, sems = refs
    parts = [refs[len(refs) - 5 * (len(firsts) - n) :][:5] for n in range(len(firsts))]
    moves = []
    for n, (first, part) in enumerate(zip(firsts, parts, strict=True)):
        there = pl.ds(first * DH, part[0].shape[1])
        pairs = ((k_hbm, part[1]), (v_hbm, part[2]), (q_hbm, part[0]), (g_hbm, part[3]))
        moves.append([pltpu.make_async_copy(src.at[:, there], dst, sems.at[n, i]) for i, (src, dst) in enumerate(pairs)])
        for move in moves[-1]:
            move.start()
    for part, own in zip(parts, moves, strict=True):
        q_ref, k_ref, v_ref, g_ref, state_ref = part
        size = state_ref.shape[1]
        cols = [slice(h * DH, (h + 1) * DH) for h in range(size)]
        own[0].wait()
        own[1].wait()
        for h in range(size):
            state_ref[0, h] = dot(k_ref[:, cols[h]], v_ref[:, cols[h]], ROWS)
        own[2].wait()
        own[3].wait()
        for h in range(size):
            state_ref[1, h] = dot(q_ref[:, cols[h]], g_ref[:, cols[h]], ROWS)


def load(arrays, firsts, size, after):
    rows = arrays[0].shape[0]
    part = [pltpu.VMEM((rows, size * DH), BF16)] * 4 + [pltpu.VMEM((2, size, DH, DH), F32)]
    return pl.pallas_call(
        functools.partial(load_kernel, firsts),
        in_specs=[HBM] * 4 + [VMEM] * len(after),
        out_specs=[VMEM] * (5 * len(firsts)),
        out_shape=part * len(firsts),
        scratch_shapes=[pltpu.SemaphoreType.DMA((len(firsts), 4))],
        compiler_params=PARAMS,
        cost_estimate=cost(1.5 + 0.5 * len(firsts)),
        name="load",
    )(*[pltpu.with_memory_space_constraint(a, pltpu.HBM) for a in arrays], *kept(after))


def within_kernel(tile, first, *refs):
    q_ref, k_ref, v_ref, g_ref = refs[:4]
    attended_ref, query_ref, key_ref, value_ref = refs[-4:]
    rows, width = attended_ref.shape
    count = rows // tile
    causal = lax.broadcasted_iota(jnp.int32, (tile, tile), 1) <= lax.broadcasted_iota(jnp.int32, (tile, tile), 0)

    @pl.loop(0, width // DH)
    def _(h):
        lanes, source = (pl.ds(pl.multiple_of(n * DH, DH), DH) for n in (h, first + h))
        at = [pl.ds(i * tile, tile) for i in range(count)]
        q, k, v, g = ([ref[a, source] for a in at] for ref in (q_ref, k_ref, v_ref, g_ref))
        attn, grads = {}, {}
        for i in range(count):
            for j in range(i + 1):
                a, b = dot(q[i], k[j], LANES), dot(g[i], v[j], LANES)
                if i == j:
                    a, b = jnp.where(causal, a, 0.0), jnp.where(causal, b, 0.0)
                attn[i, j], grads[i, j] = a.astype(BF16), b.astype(BF16)
        for i in range(count):
            attended_ref[at[i], lanes] = sum(dot(attn[i, j], v[j], PLAIN) for j in range(i + 1))
            query_ref[at[i], lanes] = sum(dot(grads[i, j], k[j], PLAIN) for j in range(i + 1))
        for j in range(count):
            key_ref[at[j], lanes] = sum(dot(grads[i, j], q[i], ROWS) for i in range(j, count))
            value_ref[at[j], lanes] = sum(dot(attn[i, j], g[i], ROWS) for i in range(j, count))


def within(run, first, width, after):
    rows = run[0].shape[0]
    return pl.pallas_call(
        functools.partial(within_kernel, min(rows, 256), first),
        in_specs=[VMEM] * (4 + len(after)),
        out_specs=[VMEM] * 4,
        out_shape=[pltpu.VMEM((rows, width), F32)] * 4,
        compiler_params=PARAMS,
        cost_estimate=cost(1.5),
        name="within",
    )(*kept(run), *kept(after))


def mix(function, shape, arrays, after, name):
    def kernel(*refs):
        row, column = spot()
        function(row, column, refs[: len(arrays)], refs[-1])

    return pl.pallas_call(
        kernel,
        in_specs=[VMEM] * (len(arrays) + len(after)),
        out_specs=VMEM,
        out_shape=pltpu.VMEM(shape, F32),
        compiler_params=PARAMS,
        cost_estimate=cost(3),
        name=name,
    )(*kept(arrays), *kept(after))


def across_kernel(turn, chain, jobs, *refs):
    *outs, token_ref, done_ref, sems = refs[-7:]
    row, column = spot()
    ready = []
    for total, first, pieces, count in jobs:
        run, refs = refs[:4], refs[4:]
        parts, refs = [refs[4 * n : 4 * n + 4] for n in range(pieces)], refs[4 * pieces :]
        sources, refs = refs[:count], refs[count:]
        ready.append((run, parts, first, [value.astype(BF16) for value in total(row, column, sources)]))
    _, slots, rows, width = done_ref.shape
    block = min(rows, ACROSS_ROWS)

    def copy(n, i, start, out):
        here = pl.ds(start, block)
        there = out.at[here, pl.ds(ready[n][2] * DH, width)]
        return pltpu.make_async_copy(done_ref.at[n, i, here], there, sems.at[n, i, start // block])

    def write(base):
        for n, ((q_ref, k_ref, v_ref, g_ref), parts, _, states) in enumerate(ready):
            wide = width // len(parts)
            factors = ((q_ref, PLAIN), (g_ref, LANES), (v_ref, LANES), (k_ref, PLAIN))
            for start in range(0, rows, block):
                here = pl.ds(start, block)
                for i in range(slots):
                    factor, dims = factors[base + i]
                    state = states[i // 2]
                    for at in range(0, width, DH):
                        part = parts[at // wide][base + i][here, pl.ds(at % wide, DH)]
                        term = dot(factor[here, pl.ds(at, DH)], state[at // DH], dims)
                        done_ref[n, i, here, pl.ds(at, DH)] = (part + term).astype(BF16)
                    copy(n, i, start, outs[base + i]).start()

    if turn is None:
        write(0)
    else:
        upper = (row < chain // 2) == (turn == 0)
        pl.when(upper)(lambda: write(0))
        pl.when(jnp.logical_not(upper))(lambda: write(2))
    token_ref[...] = jnp.zeros_like(token_ref)
    for n in range(len(ready)):
        for start in range(0, rows, block):
            for i in range(slots):
                copy(n, i, start, outs[i]).wait()


def across(jobs, turn, chain, outs, shape, size, after):
    held = () if outs is None else tuple(outs)
    arrays = [a for _, _, run, parts, sources in jobs for a in [*run, *sum(map(list, parts), []), *sources]]
    slots = 4 if turn is None else 2
    *outs, token = pl.pallas_call(
        functools.partial(
            across_kernel,
            turn,
            chain,
            [(total, first, len(parts), len(sources)) for total, first, _, parts, sources in jobs],
        ),
        in_specs=[VMEM] * len(arrays) + [HBM] * len(held) + [VMEM] * len(after),
        out_specs=[HBM] * 4 + [VMEM],
        out_shape=[jax.ShapeDtypeStruct(shape, BF16)] * 4 + [pltpu.VMEM((8, DH), F32)],
        input_output_aliases={len(arrays) + i: i for i in range(len(held))},
        scratch_shapes=[
            pltpu.VMEM((len(jobs), slots, shape[0], size * DH), BF16),
            pltpu.SemaphoreType.DMA((len(jobs), slots, max(1, shape[0] // ACROSS_ROWS))),
        ],
        compiler_params=PARAMS,
        cost_estimate=cost(0.4 * slots * len(jobs)),
        name="across",
    )(*kept(arrays), *held, *kept(after))
    return outs, token


def body(*arrays):
    heads = arrays[0].shape[1] // DH
    runs, groups_of_heads = lax.axis_size("ctx"), lax.axis_size("seq")
    chain = runs // 2
    relay = chain == 4
    parts = 4
    size = heads // parts
    shape = (size, DH, DH)
    run = [[None] * 4 for _ in range(parts)]
    own = [None] * parts
    pieces = min(size, 2)
    local = [[None] * pieces for _ in range(parts)]
    got, turns, swapped = {}, {}, {}
    last, opening = [], []
    pair = [(r, r ^ 1) for r in range(runs)]

    def early(row):
        return row < chain // 2

    def near(row, column):
        return ((row == 0) & (column == 0)) | ((row == chain - 1) & (column == 1))

    def end(row):
        return (row == 0) | (row == chain - 1)

    def far(row, column):
        return end(row) & jnp.logical_not(near(row, column))

    def swap(parity):
        perm = []
        for r in range(runs):
            z, c = r // 2, r % 2
            mate = z + 1 if z % 2 == parity else z - 1
            for s in range(groups_of_heads):
                if 0 <= mate < chain:
                    to = (2 * mate + c) * groups_of_heads + s
                else:
                    to = r * groups_of_heads + (s ^ 1)
                perm.append((r * groups_of_heads + s, to))
        return perm

    def arrival(p, z, way):
        if way == 0:
            return None if z == 0 else ((z - 1) % 2, p + z - 1)
        return None if z == chain - 1 else (z % 2, p + chain - 2 - z)

    def bring(*chosen):
        found = load(arrays, [p * size for p in chosen], size, last)
        for n, p in enumerate(chosen):
            *run[p], own[p] = found[5 * n : 5 * n + 5]
        last[:] = [own[chosen[0]]]

    def begin():
        opening[:] = first_states(arrays, [p * size for p in (0, 2, 3)], size, chain)
        last[:] = [opening[0]]

    def inside(p, piece):
        wide = max(1, size // 2)
        local[p][piece] = within(run[p], piece * wide, wide * DH, last)
        last[:] = [local[p][piece][0]]

    def share(turn):
        if opening and not turn:
            turns[0] = lax.ppermute(opening[1], "ctx", pair)
            return
        values = [own[2], own[3]]
        if turn and relay:
            values += [own[0], got[0, 0]]

        def function(row, column, refs, out):
            for n in range(2):
                first, then = refs[n][0], refs[n][1]
                value = jnp.where(early(row), *((then, first) if turn else (first, then)))
                if turn and relay:
                    mine = jnp.where(early(row), refs[2][0], refs[2][1])
                    value = jnp.where(near(row, column), mine + refs[3][...] if n else mine, value)
                    if n:
                        value = jnp.where(far(row, column), mine, value)
                out[n] = value

        payload = mix(function, (2,) + shape, values, last, "share")
        last[:] = [payload]
        turns[turn] = lax.ppermute(payload, "ctx", pair)

    def keys_of(p, turn):
        places = [(z, way) for z in range(chain) for way in range(2) if turn in (None, turn_of(way, z))]
        return sorted({arrival(p, z, way) for z, way in places} - {None})

    def turn_of(way, z):
        return 0 if early(z) == (way == 0) else 1

    def trade(p, turn=None):
        turn = 1 if relay and p == 0 else turn
        keys = keys_of(p, turn)
        late = relay and p == 1 and turn == 0
        values = [own[p]] + [got[k] for k in keys] + ([own[3]] if late else [])

        def function(row, column, refs, out):
            sums = []
            for way in range(2):
                value = jnp.where(column == way, refs[0][way], 0.0) + chained(p, way, row, refs[1:], keys)
                if late:
                    spare = (row == (0, chain - 1)[way]) & (column == 1 - way)
                    value = jnp.where(spare, refs[-1][1 - way], value)
                sums.append(value)
            if turn is None:
                out[0], out[1] = sums
            else:
                out[...] = jnp.where(early(row) == (turn == 0), *sums)

        payload = mix(function, (2,) + shape if turn is None else shape, values, last, "trade")
        last[:] = [payload]
        swapped[p, turn] = lax.ppermute(payload, "ctx", pair)

    def chained(p, way, row, refs, keys):
        total = jnp.zeros(shape, F32)
        for key, ref in zip(keys, refs):
            places = [z for z in range(chain) if arrival(p, z, way) == key]
            if places:
                total = jnp.where(any_of(row, places), ref[...], total)
        return total

    def hop(parity, slot):
        groups = {}
        for link in range(parity, chain - 1, 2):
            for way, p, z in ((0, slot - link, link), (1, slot - (chain - 2 - link), link + 1)):
                if 0 <= p < parts:
                    groups.setdefault((p, arrival(p, z, way)), ([], []))[way].append(z)
        if not groups:
            return
        forward = relay and parity == 0 and slot == 4
        names = []
        for (p, key), ways in groups.items():
            names.append(("own", p))
            if p >= 2:
                names += [("turns", turn_of(way, z)) for way in range(2) for z in ways[way]]
            if key is not None:
                names.append(("got", key))
        if forward:
            names.append(("turns", 1))
        names = list(dict.fromkeys(names))
        tables = {"own": own, "turns": turns, "got": got}
        values = [tables[kind][key] for kind, key in names]

        def function(row, column, refs, out):
            refs = dict(zip(names, refs, strict=True))

            def state(p, way, rows):
                value = refs["own", p][way]
                if p >= 2:
                    found = {turn_of(way, z) for z in rows}
                    ways = [refs["turns", turn][p - 2] if turn in found else None for turn in range(2)]
                    if len(found) == 2:
                        other = jnp.where(early(row) == (way == 0), *ways)
                    else:
                        other = ways[found.pop()]
                    value = value + other
                return value

            payload = None
            for (p, key), (up, down) in groups.items():
                if up and down:
                    rising = early(row) if relay and slot == 0 else any_of(row, up)
                    value = jnp.where(rising, state(p, 0, up), state(p, 1, down))
                else:
                    value = state(p, 0, up) if up else state(p, 1, down)
                if key is not None:
                    value = value + refs["got", key][...]
                payload = value if payload is None else jnp.where(any_of(row, up + down), value, payload)
            if forward:
                payload = jnp.where(end(row), refs["turns", 1][1], payload)
            out[...] = payload

        if opening and (parity, slot) == (0, 0):
            payload = opening[0]
        else:
            payload = mix(function, shape, values, last, "hop")
            last[:] = [payload]
        got[parity, slot] = lax.ppermute(payload, ("ctx", "seq"), swap(parity))

    outs = [None]

    def finish(turn, *chosen):
        jobs = []
        for p in chosen:
            keys = keys_of(p, turn)
            values = {("got", k): got[k] for k in keys}
            if p >= 2:
                values |= {("turns", n): turns[n] for n in range(2) if turn in (None, n)}
            elif relay and p == 1:
                values |= {("swapped", (1, n)): swapped[1, n] for n in range(2) if turn in (None, n)}
            elif relay:
                values |= {("swapped", (0, 1)): swapped[0, 1], ("turns", 1): turns[1], ("got", (0, 4)): got[0, 4]}
            else:
                values["swapped", (p, None)] = swapped[p, None]
            if relay and p == 3 and turn != 0:
                values["swapped", (1, 0)] = swapped[1, 0]

            def total(row, column, refs, p=p, keys=keys, names=tuple(values)):
                refs = dict(zip(names, refs, strict=True))
                sums = []
                for way in range(2):
                    head, tail = (0, chain - 1) if way == 0 else (chain - 1, 0)

                    def chosen_of(kind, pick):
                        if turn is not None:
                            return pick(refs[kind(turn)])
                        return jnp.where(early(row) == (way == 0), pick(refs[kind(0)]), pick(refs[kind(1)]))

                    if p >= 2:
                        extra = chosen_of(lambda n: ("turns", n), lambda ref: ref[p - 2])
                        if relay and p == 3 and turn != 0:
                            extra = jnp.where(row == tail, refs["swapped", (1, 0)][...], extra)
                        extra = jnp.where(column == 1 - way, extra, 0.0)
                    elif relay and p == 1:
                        extra = chosen_of(lambda n: ("swapped", (1, n)), lambda ref: ref[...])
                    elif relay:
                        extra = jnp.where(early(row) == (way == 0), refs["got", (0, 4)][...], refs["swapped", (0, 1)][...])
                        extra = jnp.where(row == head, refs["turns", 1][0], extra)
                    else:
                        extra = refs["swapped", (p, None)][way]
                    if p < 2:
                        extra = jnp.where((row == head) & (column == way), 0.0, extra)
                    sums.append(extra + chained(p, way, row, [refs["got", k] for k in keys], keys))
                return sums if turn is None else [jnp.where(early(row) == (turn == 0), *sums)]

            jobs.append((total, p * size, run[p], local[p], list(values.values())))
        outs[0], token = across(jobs, turn, chain, outs[0], arrays[0].shape, size, last)
        last[:] = [token]

    steps = {"F": begin, "L": bring, "S": share, "X": trade, "E": functools.partial(hop, 0), "O": functools.partial(hop, 1), "W": inside, "A": functools.partial(finish, None)}
    steps |= {"B": functools.partial(finish, 0), "C": functools.partial(finish, 1)}
    order = [(name[0], [int(n) for n in name[1:]]) for name in ORDER]
    if chain != 4:
        order = [("L", [2, 3]), ("L", [0, 1]), ("S", [0]), ("S", [1])]
        order += [("W", [p, n]) for p in range(parts) for n in range(pieces)]
        order += [(kind, [t]) for t in range(parts + chain - 2) for kind in "EO"]
        order += [("X", [0]), ("X", [1]), ("A", [2, 3]), ("A", [0, 1])]
    for kind, numbers in order:
        steps[kind](*numbers)
    return tuple(outs[0])


def solution(mesh):
    spec = P("ctx", "seq")
    return jax.shard_map(body, mesh=mesh, in_specs=(spec,) * 4, out_specs=(spec,) * 4, check_vma=False)
```
